32 devices in a mesh: row: 8 (over z, core), col: 4 (over y, x).
Axes of the slice: x: 2, y: 2, z: 4, core: 2. Of those that a mesh axis runs over, the one named last changes fastest.
Arguments:
- pair: bfloat16 [128, 128, 128], P('row', 'col'), may hold values from -6 to 6
- pair_mask: int32 [128, 128], P('row', 'col'), may hold values 0 or 1
- in_weights: bfloat16 [128, 512], replicated, may hold values from -0.5 to 0.5
- gate_weight: bfloat16 [128, 128], replicated, may hold values from -0.5 to 0.5
- out_weight: bfloat16 [128, 128], replicated, may hold values from -0.5 to 0.5
Outputs:
- update: bfloat16 [128, 128, 128], P('row', 'col')
The draws below stay inside these ranges and needn't reach their ends.
All inputs are finite; a program needn't handle non-finite values. No bound on the sum of `pair_mask` on one device may be relied on, other than what follows from the above.
Results may differ from the reference program's by a relative error of at most 0.0078.
Values may be sent and summed in bfloat16 or wider, within the bound.
No kernel may reach another device: no remote copies, remote signals or barrier semaphores. Data moves between devices by JAX's collectives and lax.ppermute only.
A program may use at most 64 MiB of HBM per device.

```python
import jax
import jax.numpy as jnp
from jax import lax

C = 128
CH = 128
N = 128


def set_ends(result, rng, smallest, largest):
    longest = result.shape.index(max(result.shape))
    spots = []
    for shift in (0, 1):
        where = [jax.random.randint(jax.random.fold_in(rng, axis), (), 0, length) for axis, length in enumerate(result.shape)]
        where[longest] = (where[longest] + shift) % result.shape[longest]
        spots.append(tuple(where))
    return result.at[spots[0]].set(smallest).at[spots[1]].set(largest)


def block_levels(stream_key, extent, pieces, low, top_value):
    gain = 1.0
    for position, parts in pieces:
        draws = jax.random.uniform(jax.random.fold_in(jax.random.fold_in(stream_key, 6), position), (parts,), jnp.float32, low / len(pieces), top_value / len(pieces))
        gain = gain * jnp.repeat(jnp.exp(draws), extent[position] // parts).reshape((-1,) + (1,) * (len(extent) - 1 - position))
    return gain


def bell_draw(key, dims, scale, most, cuts=(), kind=jnp.bfloat16):
    result = scale * jax.random.normal(key, dims, jnp.float32)
    if cuts:
        result = result * block_levels(key, dims, cuts, -0.22, 0.18)
    return jnp.clip(result, -most, most).astype(kind)


def setup_inputs(seed: int = 0) -> dict:
    key_of = jax.random.split(jax.random.key(seed), 6)
    return {
        "pair": bell_draw(key_of[0], (N, N, C), 1.0, 6.0, ((0, 8), (1, 4))),
        "pair_mask": set_ends((jax.random.randint(key_of[1], (N, N), 0, 8) < 7).astype(jnp.int32), jax.random.fold_in(key_of[1], 1), 0, 1),
        "in_weights": bell_draw(key_of[2], (C, 4 * CH), C ** -0.5, 0.5),
        "gate_weight": bell_draw(key_of[3], (C, C), C ** -0.5, 0.5),
        "out_weight": bell_draw(key_of[4], (CH, C), CH ** -0.5, 0.5),
    }


def layer_norm(values):
    mean = lax.optimization_barrier(jnp.mean(values, axis=-1, keepdims=True))
    centred = values - mean
    var = lax.optimization_barrier(jnp.mean(centred * centred, axis=-1, keepdims=True))
    return centred * jax.lax.rsqrt(var + 1e-05)

def reference(pair, pair_mask, in_weights, gate_weight, out_weight):
    count = pair.shape[0]
    width = pair.shape[2]
    hidden = in_weights.shape[1] // 4
    normed = layer_norm(pair.astype(jnp.float32).reshape(-1, width)).astype(jnp.bfloat16)
    proj = jnp.dot(normed, in_weights, preferred_element_type=jnp.float32)
    maskf = pair_mask.reshape(-1, 1).astype(jnp.float32)
    left = (maskf * jax.nn.sigmoid(proj[:, hidden:2 * hidden]) * proj[:, :hidden]).astype(jnp.bfloat16)
    right = (maskf * jax.nn.sigmoid(proj[:, 3 * hidden:]) * proj[:, 2 * hidden:3 * hidden]).astype(jnp.bfloat16)
    left = left.reshape(count, count, hidden).astype(jnp.float32)
    right = right.reshape(count, count, hidden).astype(jnp.float32)
    tri = jnp.einsum('ikc,jkc->ijc', left, right)
    tnorm = layer_norm(tri.reshape(-1, hidden)).astype(jnp.bfloat16)
    gate = jax.nn.sigmoid(jnp.dot(normed, gate_weight, preferred_element_type=jnp.float32))
    update = gate * jnp.dot(tnorm, out_weight, preferred_element_type=jnp.float32)
    return update.astype(jnp.bfloat16).reshape(count, count, width)
```

```python
import functools
import math

import jax
import jax.numpy as jnp
from jax import lax
from jax.experimental import pallas as pl
from jax.experimental.pallas import tpu as pltpu
from jax.sharding import PartitionSpec as P

ORDER = ("x", "y", "row")


def spread(value, axis, root):
    mine = lax.axis_index(axis) == root
    return lax.psum(jnp.where(mine, value, jnp.zeros_like(value)), axis)


def layer_norm(values, axis=-1):
    mean = jnp.mean(values, axis=axis, keepdims=True)
    centred = values - mean
    var = jnp.mean(centred * centred, axis=axis, keepdims=True)
    return centred * jax.lax.rsqrt(var + 1e-05)


def gather_rows(pair, pair_mask, in_weights, gate_weight, out_weight):
    rows_here = pair.shape[0]
    cols_here = pair.shape[1]
    width = pair.shape[2]
    hidden = in_weights.shape[1] // 4
    normed = layer_norm(pair.reshape(-1, width).astype(jnp.float32)).astype(jnp.bfloat16)
    proj = jnp.dot(normed, in_weights, preferred_element_type=jnp.float32)
    maskf = pair_mask.reshape(-1, 1).astype(jnp.float32)
    left = (maskf * jax.nn.sigmoid(proj[:, hidden : 2 * hidden]) * proj[:, :hidden]).astype(
        jnp.bfloat16
    )
    right = (
        maskf * jax.nn.sigmoid(proj[:, 3 * hidden :]) * proj[:, 2 * hidden : 3 * hidden]
    ).astype(jnp.bfloat16)
    left = left.reshape(rows_here, cols_here, hidden)
    right = right.reshape(rows_here, cols_here, hidden)
    gate = jax.nn.sigmoid(jnp.dot(normed, gate_weight, preferred_element_type=jnp.float32))
    ratio = lax.axis_size("row") // lax.axis_size("col")
    column = lax.axis_index("col")
    left_rows, right_rows = (
        lax.all_gather(left, "col", axis=1, tiled=True),
        lax.all_gather(right, "col", axis=1, tiled=True),
    )
    blocks = [spread(right_rows, "row", ratio * column + offset) for offset in range(ratio)]
    partner = jnp.concatenate(blocks, axis=0)
    tri = jnp.einsum("ikc,jkc->ijc", left_rows, partner, preferred_element_type=jnp.float32)
    tnorm = layer_norm(tri.reshape(-1, hidden)).astype(jnp.bfloat16)
    update = gate * jnp.dot(tnorm, out_weight, preferred_element_type=jnp.float32)
    return update.astype(jnp.bfloat16).reshape(rows_here, cols_here, width)


def sigmoid(values):
    return 0.5 * jnp.tanh(0.5 * values) + 0.5


def project_kernel(
    devices, mine, cols_here,
    pair_hbm, mask_hbm, weights_hbm, send_ref, normed_ref, pair_ref, mask_ref, weights_ref, done,
):
    spots = pair_ref.shape[0]
    hidden = devices * mine
    parts = 4
    copies = []
    for part in range(parts):
        lanes = pl.ds(part * hidden, hidden)
        copies.append((weights_hbm.at[:, lanes], weights_ref.at[:, lanes]))
    copies.append((mask_hbm, mask_ref))
    for part in range(parts):
        some = pl.ds(part * spots // parts, spots // parts)
        copies.append((pair_hbm.at[some], pair_ref.at[some]))
    copies = [pltpu.make_async_copy(*ends, done.at[n]) for n, ends in enumerate(copies)]
    for copy in copies:
        copy.start()
    shape = (2 * hidden, 2 * hidden)
    row, col = (lax.broadcasted_iota(jnp.int32, shape, n) for n in (0, 1))
    source = (row // mine) % 2 * hidden + row // (2 * mine) * mine + row % mine
    order = (col == source).astype(jnp.bfloat16)
    for copy in copies[:parts]:
        copy.wait()
    weights = weights_ref[...]

    def in_order(block):
        both = [weights[:, (block + n) * hidden : (block + n + 1) * hidden] for n in (0, 2)]
        return dot_t(order, jnp.concatenate(both, axis=1)).astype(jnp.bfloat16)

    values, gates = in_order(0), in_order(1)
    shape = (cols_here, spots)
    row, col = (lax.broadcasted_iota(jnp.int32, shape, n) for n in (0, 1))
    spread_cols = (col % cols_here == row).astype(jnp.bfloat16)
    copies[parts].wait()
    mask = mask_ref[...].astype(jnp.float32).astype(jnp.bfloat16)
    mask = jnp.dot(mask, spread_cols, preferred_element_type=jnp.float32)
    row, col = (lax.broadcasted_iota(jnp.int32, mask.shape, n) for n in (0, 1))
    mask = jnp.sum(jnp.where(col // cols_here == row, mask, 0.0), axis=0, keepdims=True)
    for copy in copies[parts + 1 :]:
        copy.wait()
    normed = layer_norm(pair_ref[...].astype(jnp.float32)).astype(jnp.bfloat16)
    normed_ref[...] = normed
    both = mask * sigmoid(dot_t(gates, normed)) * dot_t(values, normed)
    both = both.reshape(devices, 2 * mine, spots)
    half = spots // 2
    both = jnp.concatenate([both[:, :, :half], both[:, :, half:]], axis=1)
    send_ref[...] = both.astype(jnp.bfloat16)


def dot_t(a, b):
    return lax.dot_general(a, b, (((1,), (1,)), ((), ())), preferred_element_type=jnp.float32)


def swap_groups(tiles):
    lane = lax.broadcasted_iota(jnp.int32, tiles[0].shape, 1)
    width = tiles[0].shape[1]
    half, quarter = width // 2, width // 4
    low, even = lane < half, lane // quarter % 2 == 0
    a = [
        jnp.where(low, tiles[0], pltpu.roll(tiles[2], half, 1)),
        jnp.where(low, tiles[1], pltpu.roll(tiles[3], half, 1)),
        jnp.where(low, pltpu.roll(tiles[0], half, 1), tiles[2]),
        jnp.where(low, pltpu.roll(tiles[1], half, 1), tiles[3]),
    ]
    return [
        jnp.where(even, a[0], pltpu.roll(a[1], quarter, 1)),
        jnp.where(even, pltpu.roll(a[0], width - quarter, 1), a[1]),
        jnp.where(even, a[2], pltpu.roll(a[3], quarter, 1)),
        jnp.where(even, pltpu.roll(a[2], width - quarter, 1), a[3]),
    ]


NEAR, FAR, WIDE = 9, 17, 137


def mix_kernel(places, mine, recv_ref, send_ref, got, partner, back):
    rows = len(places[0])
    depth = 4 * mine
    for col, column in enumerate(places):
        for row, place in enumerate(column):
            block = recv_ref[place].astype(jnp.float32)
            for high in range(2):
                for middle in range(2):
                    tile = block[8 * high : 8 * high + 8, 128 * middle : 128 * middle + 128]
                    got[col, 2 * high + middle, pl.ds(NEAR * row, 8, stride=FAR), :] = tile

    def side(which, channel):
        first = FAR * (which * mine + channel)
        tiles = []
        for high in range(4):
            some = pl.ds(first, rows, stride=NEAR)
            tiles += swap_groups([got[col, high, some, :] for col in range(len(places))])
        return tiles

    for channel in range(mine):
        left = jnp.concatenate(side(0, channel), axis=0).astype(jnp.bfloat16)
        for n, tile in enumerate(side(1, channel)):
            partner[channel, pl.ds(NEAR * n, rows, stride=WIDE), :] = tile
        right = [
            partner[channel, pl.ds(WIDE * row + NEAR * n, 8, stride=NEAR), :]
            for row in range(rows)
            for n in (0, 8)
        ]
        tri = dot_t(left, jnp.concatenate(right, axis=0).astype(jnp.bfloat16))
        for high in range(4):
            tiles = [tri[(4 * high + n) * rows : (4 * high + n + 1) * rows] for n in range(4)]
            for col, tile in enumerate(swap_groups(tiles)):
                first = NEAR * (high * mine + channel)
                back[col, pl.ds(first, rows, stride=WIDE), :] = tile
    for col, column in enumerate(places):
        for row, place in enumerate(column):
            tiles = [
                back[col, pl.ds(WIDE * row + NEAR * n, 8, stride=NEAR), :]
                for n in range(0, depth, 8)
            ]
            send_ref[place] = jnp.concatenate(tiles, axis=0).astype(jnp.bfloat16)


def finish_kernel(recv_ref, gate_ref, weight_ref, out_hbm, out_ref, done):
    devices, depth, width = recv_ref.shape
    values = recv_ref[...].astype(jnp.float32).reshape(devices // 2, 2, depth // 8, 8, width)
    top = lax.broadcasted_iota(jnp.int32, (devices // 2, 8, width), 1) < 4
    weight = weight_ref[...]
    parts = []
    for n in range(depth // 8):
        one, two = values[:, 0, n], values[:, 1, n]
        parts.append(jnp.where(top, one, pltpu.roll(two, 4, 1)))
        parts.append(jnp.where(top, pltpu.roll(one, 4, 1), two))
    copies = []
    for n, part in enumerate(parts):
        part = layer_norm(part.reshape(devices * 4, width), axis=0)
        tnorm = part.T.astype(jnp.bfloat16)
        update = jnp.dot(tnorm, weight, preferred_element_type=jnp.float32)
        spots = pl.ds(n * width, width)
        out_ref[spots, :] = (gate_ref[spots, :] * update).astype(jnp.bfloat16)
        copies.append(pltpu.make_async_copy(out_ref.at[spots], out_hbm.at[spots], done.at[n]))
        copies[-1].start()
    for copy in copies:
        copy.wait()


def in_hbm(values):
    return pltpu.with_memory_space_constraint(values, pltpu.HBM)


def split_channels(pair, pair_mask, in_weights, gate_weight, out_weight):
    rows_here, cols_here, width = pair.shape
    hidden = in_weights.shape[1] // 4
    sizes = {name: lax.axis_size(name) for name in ORDER}
    steps = {name: math.prod([sizes[n] for n in ORDER[at + 1 :]]) for at, name in enumerate(ORDER)}
    rows, cols = sizes["row"], sizes["y"] * sizes["x"]
    firsts = [y * steps["y"] + x * steps["x"] for y in range(sizes["y"]) for x in range(sizes["x"])]
    devices = rows * cols
    mine = hidden // devices
    spots = rows_here * cols_here
    params = pltpu.CompilerParams(vmem_limit_bytes=32 * 2**20)
    both, normed = pl.pallas_call(
        functools.partial(project_kernel, devices, mine, cols_here),
        out_shape=(
            jax.ShapeDtypeStruct((devices, 4 * mine, spots // 2), jnp.bfloat16),
            jax.ShapeDtypeStruct((spots, width), jnp.bfloat16),
        ),
        in_specs=[pl.BlockSpec(memory_space=pltpu.HBM)] * 3,
        scratch_shapes=[
            pltpu.VMEM((spots, width), pair.dtype),
            pltpu.VMEM(pair_mask.shape, pair_mask.dtype),
            pltpu.VMEM(in_weights.shape, in_weights.dtype),
            pltpu.SemaphoreType.DMA((9,)),
        ],
        compiler_params=params,
        name="project",
    )(*(in_hbm(values) for values in (pair.reshape(spots, width), pair_mask, in_weights)))
    both = lax.all_to_all(both, ORDER, 0, 0, tiled=True)
    gate = sigmoid(jnp.dot(normed, gate_weight, preferred_element_type=jnp.float32))
    places = [[first + row * steps["row"] for row in range(rows)] for first in firsts]
    tri = pl.pallas_call(
        functools.partial(mix_kernel, places, mine),
        out_shape=jax.ShapeDtypeStruct((devices, 4 * mine, spots // 4), jnp.bfloat16),
        scratch_shapes=[
            pltpu.VMEM((cols, 4, 184, 128), jnp.float32),
            pltpu.VMEM((mine, 1096, 128), jnp.float32),
            pltpu.VMEM((cols, 1096, 128), jnp.float32),
        ],
        compiler_params=params,
        name="mix",
    )(both)
    tri = lax.all_to_all(tri, ORDER, 0, 0, tiled=True)
    update = pl.pallas_call(
        finish_kernel,
        out_shape=jax.ShapeDtypeStruct((spots, width), jnp.bfloat16),
        out_specs=pl.BlockSpec(memory_space=pltpu.HBM),
        scratch_shapes=[pltpu.VMEM((spots, width), jnp.bfloat16), pltpu.SemaphoreType.DMA((4,))],
        compiler_params=params,
        name="finish",
    )(tri, gate, out_weight)
    return update.reshape(rows_here, cols_here, width)


def fits(rows, cols, pair, hidden):
    sizes = (rows, cols, pair.shape[0] // rows, pair.shape[1] // cols, pair.shape[2])
    return sizes == (8, 4, 16, 32, 128) and hidden == 4 * rows * cols


def solution(mesh):
    def update(pair, pair_mask, in_weights, gate_weight, out_weight):
        rows, cols = mesh.shape["row"], mesh.shape["col"]
        if fits(rows, cols, pair, in_weights.shape[1] // 4):
            plan, col = split_channels, ("y", "x")
            over = jax.sharding.Mesh(mesh.devices.reshape(rows, 2, 2), ("row", *col))
        else:
            plan, col, over = gather_rows, "col", mesh
        in_specs = (P("row", col, None), P("row", col), P(), P(), P())
        out_specs = P("row", col, None)
        run = jax.shard_map(plan, mesh=over, in_specs=in_specs, out_specs=out_specs, check_vma=False)
        return run(pair, pair_mask, in_weights, gate_weight, out_weight)

    return update
```

```python
import functools
import math

import jax
import jax.numpy as jnp
from jax import lax
from jax.experimental import pallas as pl
from jax.experimental.pallas import tpu as pltpu
from jax.sharding import PartitionSpec as P

ORDER = ("x", "y", "row")


def spread(value, axis, root):
    mine = lax.axis_index(axis) == root
    return lax.psum(jnp.where(mine, value, jnp.zeros_like(value)), axis)


def layer_norm(values, axis=-1):
    mean = jnp.mean(values, axis=axis, keepdims=True)
    centred = values - mean
    var = jnp.mean(centred * centred, axis=axis, keepdims=True)
    return centred * jax.lax.rsqrt(var + 1e-05)


def gather_rows(pair, pair_mask, in_weights, gate_weight, out_weight):
    rows_here = pair.shape[0]
    cols_here = pair.shape[1]
    width = pair.shape[2]
    hidden = in_weights.shape[1] // 4
    normed = layer_norm(pair.reshape(-1, width).astype(jnp.float32)).astype(jnp.bfloat16)
    proj = jnp.dot(normed, in_weights, preferred_element_type=jnp.float32)
    maskf = pair_mask.reshape(-1, 1).astype(jnp.float32)
    left = (maskf * jax.nn.sigmoid(proj[:, hidden : 2 * hidden]) * proj[:, :hidden]).astype(
        jnp.bfloat16
    )
    right = (
        maskf * jax.nn.sigmoid(proj[:, 3 * hidden :]) * proj[:, 2 * hidden : 3 * hidden]
    ).astype(jnp.bfloat16)
    left = left.reshape(rows_here, cols_here, hidden)
    right = right.reshape(rows_here, cols_here, hidden)
    gate = jax.nn.sigmoid(jnp.dot(normed, gate_weight, preferred_element_type=jnp.float32))
    ratio = lax.axis_size("row") // lax.axis_size("col")
    column = lax.axis_index("col")
    left_rows, right_rows = (
        lax.all_gather(left, "col", axis=1, tiled=True),
        lax.all_gather(right, "col", axis=1, tiled=True),
    )
    blocks = [spread(right_rows, "row", ratio * column + offset) for offset in range(ratio)]
    partner = jnp.concatenate(blocks, axis=0)
    tri = jnp.einsum("ikc,jkc->ijc", left_rows, partner, preferred_element_type=jnp.float32)
    tnorm = layer_norm(tri.reshape(-1, hidden)).astype(jnp.bfloat16)
    update = gate * jnp.dot(tnorm, out_weight, preferred_element_type=jnp.float32)
    return update.astype(jnp.bfloat16).reshape(rows_here, cols_here, width)


def sigmoid(values):
    return 0.5 * jnp.tanh(0.5 * values) + 0.5


def project_kernel(
    devices, mine, cols_here,
    pair_hbm, mask_hbm, weights_hbm, send_ref, normed_ref, pair_ref, mask_ref, weights_ref, done,
):
    spots, width = pair_ref.shape
    hidden = devices * mine
    copies = []
    for source, target in ((pair_hbm, pair_ref), (weights_hbm, weights_ref)):
        half = source.shape[0] // 2
        copies += [(source.at[pl.ds(n, half)], target.at[pl.ds(n, half)]) for n in (0, half)]
    copies.append((mask_hbm, mask_ref))
    copies = [pltpu.make_async_copy(*ends, done.at[n]) for n, ends in enumerate(copies)]
    for copy in copies:
        copy.start()
    shape = (2 * hidden, 2 * hidden)
    row, col = (lax.broadcasted_iota(jnp.int32, shape, n) for n in (0, 1))
    source = (row // mine) % 2 * hidden + row // (2 * mine) * mine + row % mine
    order = (col == source).astype(jnp.bfloat16)
    shape = (cols_here, spots)
    row, col = (lax.broadcasted_iota(jnp.int32, shape, n) for n in (0, 1))
    spread_cols = (col % cols_here == row).astype(jnp.bfloat16)
    shape = (spots // cols_here, spots)
    row, col = (lax.broadcasted_iota(jnp.int32, shape, n) for n in (0, 1))
    own = col // cols_here == row
    for copy in copies[:2]:
        copy.wait()
    normed = layer_norm(pair_ref[...].astype(jnp.float32)).astype(jnp.bfloat16)
    normed_ref[...] = normed
    for copy in copies[2:]:
        copy.wait()
    weights = weights_ref[...]

    def in_order(block):
        both = [weights[:, (block + n) * hidden : (block + n + 1) * hidden] for n in (0, 2)]
        return dot_t(order, jnp.concatenate(both, axis=1)).astype(jnp.bfloat16)

    mask = mask_ref[...].astype(jnp.float32).astype(jnp.bfloat16)
    mask = jnp.dot(mask, spread_cols, preferred_element_type=jnp.float32)
    mask = jnp.sum(jnp.where(own, mask, 0.0), axis=0, keepdims=True)
    both = mask * sigmoid(dot_t(in_order(1), normed)) * dot_t(in_order(0), normed)
    both = both.reshape(devices, 2 * mine, spots)
    half = spots // 2
    both = jnp.concatenate([both[:, :, :half], both[:, :, half:]], axis=1)
    send_ref[...] = both.astype(jnp.bfloat16)


def dot_t(a, b):
    return lax.dot_general(a, b, (((1,), (1,)), ((), ())), preferred_element_type=jnp.float32)


def swap_groups(tiles):
    lane = lax.broadcasted_iota(jnp.int32, tiles[0].shape, 1)
    width = tiles[0].shape[1]
    half, quarter = width // 2, width // 4
    low, even = lane < half, lane // quarter % 2 == 0
    a = [
        jnp.where(low, tiles[0], pltpu.roll(tiles[2], half, 1)),
        jnp.where(low, tiles[1], pltpu.roll(tiles[3], half, 1)),
        jnp.where(low, pltpu.roll(tiles[0], half, 1), tiles[2]),
        jnp.where(low, pltpu.roll(tiles[1], half, 1), tiles[3]),
    ]
    return [
        jnp.where(even, a[0], pltpu.roll(a[1], quarter, 1)),
        jnp.where(even, pltpu.roll(a[0], width - quarter, 1), a[1]),
        jnp.where(even, a[2], pltpu.roll(a[3], quarter, 1)),
        jnp.where(even, pltpu.roll(a[2], width - quarter, 1), a[3]),
    ]


NEAR, FAR, WIDE = 9, 17, 137


def mix_kernel(places, mine, recv_ref, send_ref, got, partner, back):
    rows = len(places[0])
    depth = 4 * mine
    for col, column in enumerate(places):
        for row, place in enumerate(column):
            block = recv_ref[place].astype(jnp.float32)
            for high in range(2):
                for middle in range(2):
                    tile = block[8 * high : 8 * high + 8, 128 * middle : 128 * middle + 128]
                    got[col, 2 * high + middle, pl.ds(NEAR * row, 8, stride=FAR), :] = tile

    def side(which, channel):
        some = pl.ds(FAR * (which * mine + channel), rows, stride=NEAR)
        tiles = []
        for middle in range(2):
            some_of = [
                jnp.concatenate([got[col, middle, some, :], got[col, 2 + middle, some, :]], axis=0)
                for col in range(len(places))
            ]
            tiles += swap_groups([tile.astype(jnp.bfloat16) for tile in some_of])
        return tiles

    def spread_rows(target, first, step, tile):
        tile = tile.astype(jnp.float32)
        for high in range(2):
            some = pl.ds(NEAR * (first + high * step), rows, stride=WIDE)
            target[some, :] = tile[high * rows : (high + 1) * rows]

    channels = range(mine)
    for channel in channels:
        for n, tile in enumerate(side(1, channel)):
            spread_rows(partner.at[channel], n, 8, tile)
    lefts = [jnp.concatenate(side(0, channel), axis=0) for channel in channels]
    rights = [
        [
            partner[channel, pl.ds(WIDE * row + NEAR * n, 8, stride=NEAR), :]
            for row in range(rows)
            for n in (0, 8)
        ]
        for channel in channels
    ]
    rights = [jnp.concatenate(right, axis=0).astype(jnp.bfloat16) for right in rights]
    tris = [dot_t(left, right).astype(jnp.bfloat16) for left, right in zip(lefts, rights)]
    for channel, tri in enumerate(tris):
        for middle in range(2):
            firsts = [(4 * middle + n) * 2 * rows for n in range(4)]
            tiles = swap_groups([tri[first : first + 2 * rows] for first in firsts])
            for col, tile in enumerate(tiles):
                spread_rows(back.at[col], middle * mine + channel, 2 * mine, tile)
    for col, column in enumerate(places):
        for row, place in enumerate(column):
            tiles = [
                back[col, pl.ds(WIDE * row + NEAR * n, 8, stride=NEAR), :]
                for n in range(0, depth, 8)
            ]
            send_ref[place] = jnp.concatenate(tiles, axis=0).astype(jnp.bfloat16)


def finish_kernel(recv_ref, normed_ref, gate_weight_ref, weight_ref, out_hbm, out_ref, done):
    devices, depth, width = recv_ref.shape
    values = recv_ref[...].astype(jnp.float32).reshape(devices // 2, 2, depth // 8, 8, width)
    top = lax.broadcasted_iota(jnp.int32, (devices // 2, 8, width), 1) < 4
    weight = weight_ref[...]
    gate = sigmoid(
        jnp.dot(normed_ref[...], gate_weight_ref[...], preferred_element_type=jnp.float32)
    )
    parts = []
    for n in range(depth // 8):
        one, two = values[:, 0, n], values[:, 1, n]
        parts.append(jnp.where(top, one, pltpu.roll(two, 4, 1)))
        parts.append(jnp.where(top, pltpu.roll(one, 4, 1), two))
    copies = []
    for n, part in enumerate(parts):
        part = layer_norm(part.reshape(devices * 4, width), axis=0)
        tnorm = part.T.astype(jnp.bfloat16)
        update = jnp.dot(tnorm, weight, preferred_element_type=jnp.float32)
        spots = pl.ds(n * width, width)
        out_ref[spots, :] = (gate[n * width : (n + 1) * width] * update).astype(jnp.bfloat16)
        copies.append(pltpu.make_async_copy(out_ref.at[spots], out_hbm.at[spots], done.at[n]))
        if n % 2:
            copies[n - 1].start()
            copies[n].start()
    for copy in copies:
        copy.wait()


def in_hbm(values):
    return pltpu.with_memory_space_constraint(values, pltpu.HBM)


def split_channels(pair, pair_mask, in_weights, gate_weight, out_weight):
    rows_here, cols_here, width = pair.shape
    hidden = in_weights.shape[1] // 4
    sizes = {name: lax.axis_size(name) for name in ORDER}
    steps = {name: math.prod([sizes[n] for n in ORDER[at + 1 :]]) for at, name in enumerate(ORDER)}
    rows, cols = sizes["row"], sizes["y"] * sizes["x"]
    firsts = [y * steps["y"] + x * steps["x"] for y in range(sizes["y"]) for x in range(sizes["x"])]
    devices = rows * cols
    mine = hidden // devices
    spots = rows_here * cols_here
    params = pltpu.CompilerParams(vmem_limit_bytes=32 * 2**20)
    both, normed = pl.pallas_call(
        functools.partial(project_kernel, devices, mine, cols_here),
        out_shape=(
            jax.ShapeDtypeStruct((devices, 4 * mine, spots // 2), jnp.bfloat16),
            jax.ShapeDtypeStruct((spots, width), jnp.bfloat16),
        ),
        in_specs=[pl.BlockSpec(memory_space=pltpu.HBM)] * 3,
        scratch_shapes=[
            pltpu.VMEM((spots, width), pair.dtype),
            pltpu.VMEM(pair_mask.shape, pair_mask.dtype),
            pltpu.VMEM(in_weights.shape, in_weights.dtype),
            pltpu.SemaphoreType.DMA((5,)),
        ],
        compiler_params=params,
        name="project",
    )(*(in_hbm(values) for values in (pair.reshape(spots, width), pair_mask, in_weights)))
    both = lax.all_to_all(both, ORDER, 0, 0, tiled=True)
    places = [[first + row * steps["row"] for row in range(rows)] for first in firsts]
    tri = pl.pallas_call(
        functools.partial(mix_kernel, places, mine),
        out_shape=jax.ShapeDtypeStruct((devices, 4 * mine, spots // 4), jnp.bfloat16),
        scratch_shapes=[
            pltpu.VMEM((cols, 4, 184, 128), jnp.float32),
            pltpu.VMEM((mine, 1096, 128), jnp.float32),
            pltpu.VMEM((cols, 1096, 128), jnp.float32),
        ],
        compiler_params=params,
        name="mix",
    )(both)
    tri = lax.all_to_all(tri, ORDER, 0, 0, tiled=True)
    update = pl.pallas_call(
        finish_kernel,
        out_shape=jax.ShapeDtypeStruct((spots, width), jnp.bfloat16),
        out_specs=pl.BlockSpec(memory_space=pltpu.HBM),
        scratch_shapes=[pltpu.VMEM((spots, width), jnp.bfloat16), pltpu.SemaphoreType.DMA((4,))],
        compiler_params=params,
        name="finish",
    )(tri, normed, gate_weight, out_weight)
    return update.reshape(rows_here, cols_here, width)


def fits(rows, cols, pair, hidden):
    sizes = (rows, cols, pair.shape[0] // rows, pair.shape[1] // cols, pair.shape[2])
    return sizes == (8, 4, 16, 32, 128) and hidden == 4 * rows * cols


def solution(mesh):
    def update(pair, pair_mask, in_weights, gate_weight, out_weight):
        rows, cols = mesh.shape["row"], mesh.shape["col"]
        if fits(rows, cols, pair, in_weights.shape[1] // 4):
            plan, col = split_channels, ("y", "x")
            over = jax.sharding.Mesh(mesh.devices.reshape(rows, 2, 2), ("row", *col))
        else:
            plan, col, over = gather_rows, "col", mesh
        in_specs = (P("row", col, None), P("row", col), P(), P(), P())
        out_specs = P("row", col, None)
        run = jax.shard_map(plan, mesh=over, in_specs=in_specs, out_specs=out_specs, check_vma=False)
        return run(pair, pair_mask, in_weights, gate_weight, out_weight)

    return update
```

```python
import functools
import math

import jax
import jax.numpy as jnp
from jax import lax
from jax.experimental import pallas as pl
from jax.experimental.pallas import tpu as pltpu
from jax.sharding import PartitionSpec as P

ORDER = ("core", "x", "y", "z")


def spread(value, axis, root):
    mine = lax.axis_index(axis) == root
    return lax.psum(jnp.where(mine, value, jnp.zeros_like(value)), axis)


def layer_norm(values, axis=-1):
    mean = jnp.mean(values, axis=axis, keepdims=True)
    centred = values - mean
    var = jnp.mean(centred * centred, axis=axis, keepdims=True)
    return centred * jax.lax.rsqrt(var + 1e-05)


def gather_rows(pair, pair_mask, in_weights, gate_weight, out_weight):
    rows_here = pair.shape[0]
    cols_here = pair.shape[1]
    width = pair.shape[2]
    hidden = in_weights.shape[1] // 4
    normed = layer_norm(pair.reshape(-1, width).astype(jnp.float32)).astype(jnp.bfloat16)
    proj = jnp.dot(normed, in_weights, preferred_element_type=jnp.float32)
    maskf = pair_mask.reshape(-1, 1).astype(jnp.float32)
    left = (maskf * jax.nn.sigmoid(proj[:, hidden : 2 * hidden]) * proj[:, :hidden]).astype(
        jnp.bfloat16
    )
    right = (
        maskf * jax.nn.sigmoid(proj[:, 3 * hidden :]) * proj[:, 2 * hidden : 3 * hidden]
    ).astype(jnp.bfloat16)
    left = left.reshape(rows_here, cols_here, hidden)
    right = right.reshape(rows_here, cols_here, hidden)
    gate = jax.nn.sigmoid(jnp.dot(normed, gate_weight, preferred_element_type=jnp.float32))
    ratio = lax.axis_size("row") // lax.axis_size("col")
    column = lax.axis_index("col")
    left_rows, right_rows = (
        lax.all_gather(left, "col", axis=1, tiled=True),
        lax.all_gather(right, "col", axis=1, tiled=True),
    )
    blocks = [spread(right_rows, "row", ratio * column + offset) for offset in range(ratio)]
    partner = jnp.concatenate(blocks, axis=0)
    tri = jnp.einsum("ikc,jkc->ijc", left_rows, partner, preferred_element_type=jnp.float32)
    tnorm = layer_norm(tri.reshape(-1, hidden)).astype(jnp.bfloat16)
    update = gate * jnp.dot(tnorm, out_weight, preferred_element_type=jnp.float32)
    return update.astype(jnp.bfloat16).reshape(rows_here, cols_here, width)


def sigmoid(values):
    return 0.5 * jnp.tanh(0.5 * values) + 0.5


def project_kernel(
    devices, mine, cols_here,
    pair_hbm, mask_hbm, weights_hbm, send_ref, normed_ref, pair_ref, mask_ref, weights_ref, done,
):
    spots, width = pair_ref.shape
    hidden = devices * mine
    copies = [(mask_hbm, mask_ref)]
    for source, target in ((weights_hbm, weights_ref), (pair_hbm, pair_ref)):
        half = source.shape[0] // 2
        copies += [(source.at[pl.ds(n, half)], target.at[pl.ds(n, half)]) for n in (0, half)]
    copies = [pltpu.make_async_copy(*ends, done.at[n]) for n, ends in enumerate(copies)]
    for copy in copies:
        copy.start()
    shape = (2 * hidden, 2 * hidden)
    row, col = (lax.broadcasted_iota(jnp.int32, shape, n) for n in (0, 1))
    source = (row // mine) % 2 * hidden + row // (2 * mine) * mine + row % mine
    order = (col == source).astype(jnp.bfloat16)
    shape = (cols_here, spots)
    row, col = (lax.broadcasted_iota(jnp.int32, shape, n) for n in (0, 1))
    spread_cols = (col % cols_here == row).astype(jnp.bfloat16)
    shape = (spots // cols_here, spots)
    row, col = (lax.broadcasted_iota(jnp.int32, shape, n) for n in (0, 1))
    own = col // cols_here == row
    for copy in copies:
        copy.wait()
    weights = weights_ref[...]

    def in_order(block):
        both = [weights[:, (block + n) * hidden : (block + n + 1) * hidden] for n in (0, 2)]
        return dot_t(order, jnp.concatenate(both, axis=1)).astype(jnp.bfloat16)

    mask = mask_ref[...].astype(jnp.float32).astype(jnp.bfloat16)
    mask = jnp.dot(mask, spread_cols, preferred_element_type=jnp.float32)
    mask = jnp.sum(jnp.where(own, mask, 0.0), axis=0, keepdims=True)
    normed = layer_norm(pair_ref[...].astype(jnp.float32)).astype(jnp.bfloat16)
    normed_ref[...] = normed
    both = mask * sigmoid(dot_t(in_order(1), normed)) * dot_t(in_order(0), normed)
    both = both.reshape(devices, 2 * mine, spots)
    half = spots // 2
    both = jnp.concatenate([both[:, :, :half], both[:, :, half:]], axis=1)
    send_ref[...] = both.astype(jnp.bfloat16)


def dot_t(a, b):
    return lax.dot_general(a, b, (((1,), (1,)), ((), ())), preferred_element_type=jnp.float32)


def swap_groups(tiles):
    lane = lax.broadcasted_iota(jnp.int32, tiles[0].shape, 1)
    width = tiles[0].shape[1]
    half, quarter = width // 2, width // 4
    low, even = lane < half, lane // quarter % 2 == 0
    a = [
        jnp.where(low, tiles[0], pltpu.roll(tiles[2], half, 1)),
        jnp.where(low, tiles[1], pltpu.roll(tiles[3], half, 1)),
        jnp.where(low, pltpu.roll(tiles[0], half, 1), tiles[2]),
        jnp.where(low, pltpu.roll(tiles[1], half, 1), tiles[3]),
    ]
    return [
        jnp.where(even, a[0], pltpu.roll(a[1], quarter, 1)),
        jnp.where(even, pltpu.roll(a[0], width - quarter, 1), a[1]),
        jnp.where(even, a[2], pltpu.roll(a[3], quarter, 1)),
        jnp.where(even, pltpu.roll(a[2], width - quarter, 1), a[3]),
    ]


NEAR, FAR, WIDE = 9, 17, 137


def mix_kernel(places, mine, recv_ref, send_ref, got, partner, back):
    rows = len(places[0])
    depth = 4 * mine
    for col, column in enumerate(places):
        for row, place in enumerate(column):
            block = recv_ref[place].astype(jnp.float32)
            for high in range(2):
                for middle in range(2):
                    tile = block[8 * high : 8 * high + 8, 128 * middle : 128 * middle + 128]
                    got[col, 2 * high + middle, pl.ds(NEAR * row, 8, stride=FAR), :] = tile

    def side(which, channel):
        some = pl.ds(FAR * (which * mine + channel), rows, stride=NEAR)
        tiles = []
        for middle in range(2):
            some_of = [
                jnp.concatenate([got[col, middle, some, :], got[col, 2 + middle, some, :]], axis=0)
                for col in range(len(places))
            ]
            tiles += swap_groups([tile.astype(jnp.bfloat16) for tile in some_of])
        return tiles

    def spread_rows(target, first, step, tile):
        tile = tile.astype(jnp.float32)
        for high in range(2):
            some = pl.ds(NEAR * (first + high * step), rows, stride=WIDE)
            target[some, :] = tile[high * rows : (high + 1) * rows]

    channels = range(mine)
    for channel in channels:
        for n, tile in enumerate(side(1, channel)):
            spread_rows(partner.at[channel], n, 8, tile)
    lefts = [jnp.concatenate(side(0, channel), axis=0) for channel in channels]
    rights = [
        [
            partner[channel, pl.ds(WIDE * row + NEAR * n, 8, stride=NEAR), :]
            for row in range(rows)
            for n in (0, 8)
        ]
        for channel in channels
    ]
    rights = [jnp.concatenate(right, axis=0).astype(jnp.bfloat16) for right in rights]
    tris = [dot_t(left, right).astype(jnp.bfloat16) for left, right in zip(lefts, rights)]
    for channel, tri in enumerate(tris):
        for middle in range(2):
            firsts = [(4 * middle + n) * 2 * rows for n in range(4)]
            tiles = swap_groups([tri[first : first + 2 * rows] for first in firsts])
            for col, tile in enumerate(tiles):
                spread_rows(back.at[col], middle * mine + channel, 2 * mine, tile)
    for col, column in enumerate(places):
        for row, place in enumerate(column):
            tiles = [
                back[col, pl.ds(WIDE * row + NEAR * n, 8, stride=NEAR), :]
                for n in range(0, depth, 8)
            ]
            send_ref[place] = jnp.concatenate(tiles, axis=0).astype(jnp.bfloat16)


def finish_kernel(recv_ref, normed_ref, gate_weight_ref, weight_ref, out_hbm, out_ref, done):
    devices, depth, width = recv_ref.shape
    values = recv_ref[...].astype(jnp.float32).reshape(devices // 2, 2, depth // 8, 8, width)
    top = lax.broadcasted_iota(jnp.int32, (devices // 2, 8, width), 1) < 4
    weight = weight_ref[...]
    gate = sigmoid(
        jnp.dot(normed_ref[...], gate_weight_ref[...], preferred_element_type=jnp.float32)
    )
    parts = []
    for n in range(depth // 8):
        one, two = values[:, 0, n], values[:, 1, n]
        parts.append(jnp.where(top, one, pltpu.roll(two, 4, 1)))
        parts.append(jnp.where(top, pltpu.roll(one, 4, 1), two))
    copies = []
    for n, part in enumerate(parts):
        part = layer_norm(part.reshape(devices * 4, width), axis=0)
        tnorm = part.T.astype(jnp.bfloat16)
        update = jnp.dot(tnorm, weight, preferred_element_type=jnp.float32)
        spots = pl.ds(n * width, width)
        out_ref[spots, :] = (gate[n * width : (n + 1) * width] * update).astype(jnp.bfloat16)
        copies.append(pltpu.make_async_copy(out_ref.at[spots], out_hbm.at[spots], done.at[n]))
    for copy in copies:
        copy.start()
    for copy in copies:
        copy.wait()


def in_hbm(values):
    return pltpu.with_memory_space_constraint(values, pltpu.HBM)


def split_channels(pair, pair_mask, in_weights, gate_weight, out_weight):
    rows_here, cols_here, width = pair.shape
    hidden = in_weights.shape[1] // 4
    sizes = {name: lax.axis_size(name) for name in ORDER}
    steps = {name: math.prod([sizes[n] for n in ORDER[at + 1 :]]) for at, name in enumerate(ORDER)}

    def offsets(slow, fast):
        pairs = [(m, n) for m in range(sizes[slow]) for n in range(sizes[fast])]
        return [m * steps[slow] + n * steps[fast] for m, n in pairs]

    in_rows, in_cols = offsets("z", "core"), offsets("y", "x")
    places = [[first + row for row in in_rows] for first in in_cols]
    rows, cols = len(in_rows), len(in_cols)
    devices = rows * cols
    mine = hidden // devices
    spots = rows_here * cols_here
    params = pltpu.CompilerParams(vmem_limit_bytes=32 * 2**20)
    both, normed = pl.pallas_call(
        functools.partial(project_kernel, devices, mine, cols_here),
        out_shape=(
            jax.ShapeDtypeStruct((devices, 4 * mine, spots // 2), jnp.bfloat16),
            jax.ShapeDtypeStruct((spots, width), jnp.bfloat16),
        ),
        in_specs=[pl.BlockSpec(memory_space=pltpu.HBM)] * 3,
        scratch_shapes=[
            pltpu.VMEM((spots, width), pair.dtype),
            pltpu.VMEM(pair_mask.shape, pair_mask.dtype),
            pltpu.VMEM(in_weights.shape, in_weights.dtype),
            pltpu.SemaphoreType.DMA((5,)),
        ],
        compiler_params=params,
        name="project",
    )(*(in_hbm(values) for values in (pair.reshape(spots, width), pair_mask, in_weights)))
    both = lax.all_to_all(both, ORDER, 0, 0, tiled=True)
    tri = pl.pallas_call(
        functools.partial(mix_kernel, places, mine),
        out_shape=jax.ShapeDtypeStruct((devices, 4 * mine, spots // 4), jnp.bfloat16),
        scratch_shapes=[
            pltpu.VMEM((cols, 4, 184, 128), jnp.float32),
            pltpu.VMEM((mine, 1096, 128), jnp.float32),
            pltpu.VMEM((cols, 1096, 128), jnp.float32),
        ],
        compiler_params=params,
        name="mix",
    )(both)
    tri = lax.all_to_all(tri, ORDER, 0, 0, tiled=True)
    update = pl.pallas_call(
        finish_kernel,
        out_shape=jax.ShapeDtypeStruct((spots, width), jnp.bfloat16),
        out_specs=pl.BlockSpec(memory_space=pltpu.HBM),
        scratch_shapes=[pltpu.VMEM((spots, width), jnp.bfloat16), pltpu.SemaphoreType.DMA((4,))],
        compiler_params=params,
        name="finish",
    )(tri, normed, gate_weight, out_weight)
    return update.reshape(rows_here, cols_here, width)


def fits(rows, cols, pair, hidden):
    sizes = (rows, cols, pair.shape[0] // rows, pair.shape[1] // cols, pair.shape[2])
    return sizes == (8, 4, 16, 32, 128) and hidden == 4 * rows * cols


def solution(mesh):
    def update(pair, pair_mask, in_weights, gate_weight, out_weight):
        rows, cols = mesh.shape["row"], mesh.shape["col"]
        if fits(rows, cols, pair, in_weights.shape[1] // 4):
            plan, row, col = split_channels, ("z", "core"), ("y", "x")
            over = jax.sharding.Mesh(mesh.devices.reshape(rows // 2, 2, 2, cols // 2), row + col)
        else:
            plan, row, col, over = gather_rows, "row", "col", mesh
        in_specs = (P(row, col, None), P(row, col), P(), P(), P())
        out_specs = P(row, col, None)
        run = jax.shard_map(plan, mesh=over, in_specs=in_specs, out_specs=out_specs, check_vma=False)
        return run(pair, pair_mask, in_weights, gate_weight, out_weight)

    return update
```

```python
import functools
import math

import jax
import jax.numpy as jnp
from jax import lax
from jax.experimental import pallas as pl
from jax.experimental.pallas import tpu as pltpu
from jax.sharding import PartitionSpec as P

THERE, BACK = ("x", "y", "z", "core"), ("core", "x", "y", "z")


def spread(value, axis, root):
    mine = lax.axis_index(axis) == root
    return lax.psum(jnp.where(mine, value, jnp.zeros_like(value)), axis)


def layer_norm(values, axis=-1):
    mean = jnp.mean(values, axis=axis, keepdims=True)
    centred = values - mean
    var = jnp.mean(centred * centred, axis=axis, keepdims=True)
    return centred * jax.lax.rsqrt(var + 1e-05)


def gather_rows(pair, pair_mask, in_weights, gate_weight, out_weight):
    rows_here = pair.shape[0]
    cols_here = pair.shape[1]
    width = pair.shape[2]
    hidden = in_weights.shape[1] // 4
    normed = layer_norm(pair.reshape(-1, width).astype(jnp.float32)).astype(jnp.bfloat16)
    proj = jnp.dot(normed, in_weights, preferred_element_type=jnp.float32)
    maskf = pair_mask.reshape(-1, 1).astype(jnp.float32)
    left = (maskf * jax.nn.sigmoid(proj[:, hidden : 2 * hidden]) * proj[:, :hidden]).astype(
        jnp.bfloat16
    )
    right = (
        maskf * jax.nn.sigmoid(proj[:, 3 * hidden :]) * proj[:, 2 * hidden : 3 * hidden]
    ).astype(jnp.bfloat16)
    left = left.reshape(rows_here, cols_here, hidden)
    right = right.reshape(rows_here, cols_here, hidden)
    gate = jax.nn.sigmoid(jnp.dot(normed, gate_weight, preferred_element_type=jnp.float32))
    ratio = lax.axis_size("row") // lax.axis_size("col")
    column = lax.axis_index("col")
    left_rows, right_rows = (
        lax.all_gather(left, "col", axis=1, tiled=True),
        lax.all_gather(right, "col", axis=1, tiled=True),
    )
    blocks = [spread(right_rows, "row", ratio * column + offset) for offset in range(ratio)]
    partner = jnp.concatenate(blocks, axis=0)
    tri = jnp.einsum("ikc,jkc->ijc", left_rows, partner, preferred_element_type=jnp.float32)
    tnorm = layer_norm(tri.reshape(-1, hidden)).astype(jnp.bfloat16)
    update = gate * jnp.dot(tnorm, out_weight, preferred_element_type=jnp.float32)
    return update.astype(jnp.bfloat16).reshape(rows_here, cols_here, width)


def sigmoid(values):
    return 0.5 * jnp.tanh(0.5 * values) + 0.5


def project_kernel(
    devices, mine, cols_here,
    pair_hbm, mask_hbm, weights_hbm, send_ref, normed_ref, pair_ref, mask_ref, weights_ref, done,
):
    spots, width = pair_ref.shape
    hidden = devices * mine
    copies = [(mask_hbm, mask_ref)]
    for source, target in ((weights_hbm, weights_ref), (pair_hbm, pair_ref)):
        part = source.shape[0] // 4
        parts = [pl.ds(n * part, part) for n in range(4)]
        copies += [(source.at[some], target.at[some]) for some in parts]
    copies = [pltpu.make_async_copy(*ends, done.at[n]) for n, ends in enumerate(copies)]
    for copy in copies:
        copy.start()
    shape = (2 * hidden, 2 * hidden)
    row, col = (lax.broadcasted_iota(jnp.int32, shape, n) for n in (0, 1))
    source = (row // mine) % 2 * hidden + row // (2 * mine) * mine + row % mine
    order = (col == source).astype(jnp.bfloat16)
    shape = (cols_here, spots)
    row, col = (lax.broadcasted_iota(jnp.int32, shape, n) for n in (0, 1))
    spread_cols = (col % cols_here == row).astype(jnp.bfloat16)
    shape = (spots // cols_here, spots)
    row, col = (lax.broadcasted_iota(jnp.int32, shape, n) for n in (0, 1))
    own = col // cols_here == row
    for copy in copies:
        copy.wait()
    weights = weights_ref[...]

    def in_order(block):
        both = [weights[:, (block + n) * hidden : (block + n + 1) * hidden] for n in (0, 2)]
        return dot_t(order, jnp.concatenate(both, axis=1)).astype(jnp.bfloat16)

    mask = mask_ref[...].astype(jnp.float32).astype(jnp.bfloat16)
    mask = jnp.dot(mask, spread_cols, preferred_element_type=jnp.float32)
    mask = jnp.sum(jnp.where(own, mask, 0.0), axis=0, keepdims=True)
    normed = layer_norm(pair_ref[...].astype(jnp.float32)).astype(jnp.bfloat16)
    normed_ref[...] = normed
    both = mask * sigmoid(dot_t(in_order(1), normed)) * dot_t(in_order(0), normed)
    both = both.reshape(devices, 2 * mine, spots)
    half = spots // 2
    both = jnp.concatenate([both[:, :, :half], both[:, :, half:]], axis=1)
    send_ref[...] = both.astype(jnp.bfloat16)


def dot_t(a, b):
    return lax.dot_general(a, b, (((1,), (1,)), ((), ())), preferred_element_type=jnp.float32)


def swap_groups(tiles):
    lane = lax.broadcasted_iota(jnp.int32, tiles[0].shape, 1)
    width = tiles[0].shape[1]
    half, quarter = width // 2, width // 4
    low, even = lane < half, lane // quarter % 2 == 0
    a = [
        jnp.where(low, tiles[0], pltpu.roll(tiles[2], half, 1)),
        jnp.where(low, tiles[1], pltpu.roll(tiles[3], half, 1)),
        jnp.where(low, pltpu.roll(tiles[0], half, 1), tiles[2]),
        jnp.where(low, pltpu.roll(tiles[1], half, 1), tiles[3]),
    ]
    return [
        jnp.where(even, a[0], pltpu.roll(a[1], quarter, 1)),
        jnp.where(even, pltpu.roll(a[0], width - quarter, 1), a[1]),
        jnp.where(even, a[2], pltpu.roll(a[3], quarter, 1)),
        jnp.where(even, pltpu.roll(a[2], width - quarter, 1), a[3]),
    ]


NEAR, FAR, WIDE = 9, 17, 137


def mix_kernel(places, back_places, mine, recv_ref, send_ref, got, partner, back):
    rows = len(places[0])
    depth = 4 * mine
    for col, column in enumerate(places):
        for row, place in enumerate(column):
            block = recv_ref[place].astype(jnp.float32)
            for high in range(2):
                for middle in range(2):
                    tile = block[8 * high : 8 * high + 8, 128 * middle : 128 * middle + 128]
                    got[col, 2 * high + middle, pl.ds(NEAR * row, 8, stride=FAR), :] = tile

    def side(which, channel):
        some = pl.ds(FAR * (which * mine + channel), rows, stride=NEAR)
        tiles = []
        for middle in range(2):
            some_of = [
                jnp.concatenate([got[col, middle, some, :], got[col, 2 + middle, some, :]], axis=0)
                for col in range(len(places))
            ]
            tiles += swap_groups([tile.astype(jnp.bfloat16) for tile in some_of])
        return tiles

    def spread_rows(target, first, step, tile):
        tile = tile.astype(jnp.float32)
        for high in range(2):
            some = pl.ds(NEAR * (first + high * step), rows, stride=WIDE)
            target[some, :] = tile[high * rows : (high + 1) * rows]

    channels = range(mine)
    for channel in channels:
        for n, tile in enumerate(side(1, channel)):
            spread_rows(partner.at[channel], n, 8, tile)
    lefts = [jnp.concatenate(side(0, channel), axis=0) for channel in channels]
    rights = [
        [
            partner[channel, pl.ds(WIDE * row + NEAR * n, 8, stride=NEAR), :]
            for row in range(rows)
            for n in (0, 8)
        ]
        for channel in channels
    ]
    rights = [jnp.concatenate(right, axis=0).astype(jnp.bfloat16) for right in rights]
    tris = [dot_t(left, right).astype(jnp.bfloat16) for left, right in zip(lefts, rights)]
    for channel, tri in enumerate(tris):
        for middle in range(2):
            firsts = [(4 * middle + n) * 2 * rows for n in range(4)]
            tiles = swap_groups([tri[first : first + 2 * rows] for first in firsts])
            for col, tile in enumerate(tiles):
                spread_rows(back.at[col], middle * mine + channel, 2 * mine, tile)
    for col, column in enumerate(back_places):
        for row, place in enumerate(column):
            tiles = [
                back[col, pl.ds(WIDE * row + NEAR * n, 8, stride=NEAR), :]
                for n in range(0, depth, 8)
            ]
            send_ref[place] = jnp.concatenate(tiles, axis=0).astype(jnp.bfloat16)


def finish_kernel(owners, recv_ref, normed_ref, gate_weight_ref, weight_ref, out_hbm, out_ref, done):
    devices, depth, width = recv_ref.shape
    values = jnp.stack([recv_ref[place] for place in owners]).astype(jnp.float32)
    values = values.reshape(devices // 2, 2, depth // 8, 8, width)
    top = lax.broadcasted_iota(jnp.int32, (devices // 2, 8, width), 1) < 4
    weight = weight_ref[...]
    gate = sigmoid(
        jnp.dot(normed_ref[...], gate_weight_ref[...], preferred_element_type=jnp.float32)
    )
    parts = []
    for n in range(depth // 8):
        one, two = values[:, 0, n], values[:, 1, n]
        parts.append(jnp.where(top, one, pltpu.roll(two, 4, 1)))
        parts.append(jnp.where(top, pltpu.roll(one, 4, 1), two))
    copies = []
    for n, part in enumerate(parts):
        part = layer_norm(part.reshape(devices * 4, width), axis=0)
        tnorm = part.T.astype(jnp.bfloat16)
        update = jnp.dot(tnorm, weight, preferred_element_type=jnp.float32)
        spots = pl.ds(n * width, width)
        out_ref[spots, :] = (gate[n * width : (n + 1) * width] * update).astype(jnp.bfloat16)
        copies.append(pltpu.make_async_copy(out_ref.at[spots], out_hbm.at[spots], done.at[n]))
    for copy in copies:
        copy.start()
    for copy in copies:
        copy.wait()


def in_hbm(values):
    return pltpu.with_memory_space_constraint(values, pltpu.HBM)


def places_of(order):
    sizes = {name: lax.axis_size(name) for name in order}
    steps = {name: math.prod([sizes[n] for n in order[at + 1 :]]) for at, name in enumerate(order)}

    def offsets(slow, fast):
        pairs = [(m, n) for m in range(sizes[slow]) for n in range(sizes[fast])]
        return [m * steps[slow] + n * steps[fast] for m, n in pairs]

    return [[first + row for row in offsets("z", "core")] for first in offsets("y", "x")]


def split_channels(pair, pair_mask, in_weights, gate_weight, out_weight):
    rows_here, cols_here, width = pair.shape
    hidden = in_weights.shape[1] // 4
    places, back_places = places_of(THERE), places_of(BACK)
    rows, cols = len(places[0]), len(places)
    owners = sorted(zip(sum(places, []), sum(back_places, [])))
    devices = rows * cols
    mine = hidden // devices
    spots = rows_here * cols_here
    params = pltpu.CompilerParams(vmem_limit_bytes=32 * 2**20)
    both, normed = pl.pallas_call(
        functools.partial(project_kernel, devices, mine, cols_here),
        out_shape=(
            jax.ShapeDtypeStruct((devices, 4 * mine, spots // 2), jnp.bfloat16),
            jax.ShapeDtypeStruct((spots, width), jnp.bfloat16),
        ),
        in_specs=[pl.BlockSpec(memory_space=pltpu.HBM)] * 3,
        scratch_shapes=[
            pltpu.VMEM((spots, width), pair.dtype),
            pltpu.VMEM(pair_mask.shape, pair_mask.dtype),
            pltpu.VMEM(in_weights.shape, in_weights.dtype),
            pltpu.SemaphoreType.DMA((9,)),
        ],
        compiler_params=params,
        name="project",
    )(*(in_hbm(values) for values in (pair.reshape(spots, width), pair_mask, in_weights)))
    both = lax.all_to_all(both, THERE, 0, 0, tiled=True)
    tri = pl.pallas_call(
        functools.partial(mix_kernel, places, back_places, mine),
        out_shape=jax.ShapeDtypeStruct((devices, 4 * mine, spots // 4), jnp.bfloat16),
        scratch_shapes=[
            pltpu.VMEM((cols, 4, 184, 128), jnp.float32),
            pltpu.VMEM((mine, 1096, 128), jnp.float32),
            pltpu.VMEM((cols, 1096, 128), jnp.float32),
        ],
        compiler_params=params,
        name="mix",
    )(both)
    tri = lax.all_to_all(tri, BACK, 0, 0, tiled=True)
    update = pl.pallas_call(
        functools.partial(finish_kernel, [place for _, place in owners]),
        out_shape=jax.ShapeDtypeStruct((spots, width), jnp.bfloat16),
        out_specs=pl.BlockSpec(memory_space=pltpu.HBM),
        scratch_shapes=[pltpu.VMEM((spots, width), jnp.bfloat16), pltpu.SemaphoreType.DMA((4,))],
        compiler_params=params,
        name="finish",
    )(tri, normed, gate_weight, out_weight)
    return update.reshape(rows_here, cols_here, width)


def fits(rows, cols, pair, hidden):
    sizes = (rows, cols, pair.shape[0] // rows, pair.shape[1] // cols, pair.shape[2])
    return sizes == (8, 4, 16, 32, 128) and hidden == 4 * rows * cols


def solution(mesh):
    def update(pair, pair_mask, in_weights, gate_weight, out_weight):
        rows, cols = mesh.shape["row"], mesh.shape["col"]
        if fits(rows, cols, pair, in_weights.shape[1] // 4):
            plan, row, col = split_channels, ("z", "core"), ("y", "x")
            over = jax.sharding.Mesh(mesh.devices.reshape(rows // 2, 2, 2, cols // 2), row + col)
        else:
            plan, row, col, over = gather_rows, "row", "col", mesh
        in_specs = (P(row, col, None), P(row, col), P(), P(), P())
        out_specs = P(row, col, None)
        run = jax.shard_map(plan, mesh=over, in_specs=in_specs, out_specs=out_specs, check_vma=False)
        return run(pair, pair_mask, in_weights, gate_weight, out_weight)

    return update
```

```python
import functools
import math

import jax
import jax.numpy as jnp
from jax import lax
from jax.experimental import pallas as pl
from jax.experimental.pallas import tpu as pltpu
from jax.sharding import PartitionSpec as P

THERE, BACK = ("x", "y", "z", "core"), ("core", "x", "y", "z")


def spread(value, axis, root):
    mine = lax.axis_index(axis) == root
    return lax.psum(jnp.where(mine, value, jnp.zeros_like(value)), axis)


def layer_norm(values, axis=-1):
    mean = jnp.mean(values, axis=axis, keepdims=True)
    centred = values - mean
    var = jnp.mean(centred * centred, axis=axis, keepdims=True)
    return centred * jax.lax.rsqrt(var + 1e-05)


def gather_rows(pair, pair_mask, in_weights, gate_weight, out_weight):
    rows_here = pair.shape[0]
    cols_here = pair.shape[1]
    width = pair.shape[2]
    hidden = in_weights.shape[1] // 4
    normed = layer_norm(pair.reshape(-1, width).astype(jnp.float32)).astype(jnp.bfloat16)
    proj = jnp.dot(normed, in_weights, preferred_element_type=jnp.float32)
    maskf = pair_mask.reshape(-1, 1).astype(jnp.float32)
    left = (maskf * jax.nn.sigmoid(proj[:, hidden : 2 * hidden]) * proj[:, :hidden]).astype(
        jnp.bfloat16
    )
    right = (
        maskf * jax.nn.sigmoid(proj[:, 3 * hidden :]) * proj[:, 2 * hidden : 3 * hidden]
    ).astype(jnp.bfloat16)
    left = left.reshape(rows_here, cols_here, hidden)
    right = right.reshape(rows_here, cols_here, hidden)
    gate = jax.nn.sigmoid(jnp.dot(normed, gate_weight, preferred_element_type=jnp.float32))
    ratio = lax.axis_size("row") // lax.axis_size("col")
    column = lax.axis_index("col")
    left_rows, right_rows = (
        lax.all_gather(left, "col", axis=1, tiled=True),
        lax.all_gather(right, "col", axis=1, tiled=True),
    )
    blocks = [spread(right_rows, "row", ratio * column + offset) for offset in range(ratio)]
    partner = jnp.concatenate(blocks, axis=0)
    tri = jnp.einsum("ikc,jkc->ijc", left_rows, partner, preferred_element_type=jnp.float32)
    tnorm = layer_norm(tri.reshape(-1, hidden)).astype(jnp.bfloat16)
    update = gate * jnp.dot(tnorm, out_weight, preferred_element_type=jnp.float32)
    return update.astype(jnp.bfloat16).reshape(rows_here, cols_here, width)


def sigmoid(values):
    return 0.5 * jnp.tanh(0.5 * values) + 0.5


def project_kernel(
    devices, mine, cols_here,
    pair_hbm, mask_hbm, weights_hbm, send_ref, normed_ref, pair_ref, mask_ref, weights_ref, done,
):
    spots, width = pair_ref.shape
    hidden = devices * mine
    copies = [(mask_hbm, mask_ref)]
    for source, target in ((weights_hbm, weights_ref), (pair_hbm, pair_ref)):
        part = source.shape[0] // 4
        parts = [pl.ds(n * part, part) for n in range(4)]
        copies += [(source.at[some], target.at[some]) for some in parts]
    copies = [pltpu.make_async_copy(*ends, done.at[n]) for n, ends in enumerate(copies)]
    for copy in copies:
        copy.start()
    shape = (2 * hidden, 2 * hidden)
    row, col = (lax.broadcasted_iota(jnp.int32, shape, n) for n in (0, 1))
    source = (row // mine) % 2 * hidden + row // (2 * mine) * mine + row % mine
    order = (col == source).astype(jnp.bfloat16)
    shape = (cols_here, spots)
    row, col = (lax.broadcasted_iota(jnp.int32, shape, n) for n in (0, 1))
    spread_cols = (col % cols_here == row).astype(jnp.bfloat16)
    shape = (spots // cols_here, spots)
    row, col = (lax.broadcasted_iota(jnp.int32, shape, n) for n in (0, 1))
    own = col // cols_here == row
    for copy in copies:
        copy.wait()
    weights = weights_ref[...]

    def in_order(block):
        both = [weights[:, (block + n) * hidden : (block + n + 1) * hidden] for n in (0, 2)]
        return dot_t(order, jnp.concatenate(both, axis=1)).astype(jnp.bfloat16)

    mask = mask_ref[...].astype(jnp.float32).astype(jnp.bfloat16)
    mask = jnp.dot(mask, spread_cols, preferred_element_type=jnp.float32)
    mask = jnp.sum(jnp.where(own, mask, 0.0), axis=0, keepdims=True)
    normed = layer_norm(pair_ref[...].astype(jnp.float32)).astype(jnp.bfloat16)
    normed_ref[...] = normed
    both = mask * sigmoid(dot_t(in_order(1), normed)) * dot_t(in_order(0), normed)
    both = both.reshape(devices, 2 * mine, spots)
    half = spots // 2
    both = jnp.concatenate([both[:, :, :half], both[:, :, half:]], axis=1)
    send_ref[...] = both.astype(jnp.bfloat16)


def dot_t(a, b):
    return lax.dot_general(a, b, (((1,), (1,)), ((), ())), preferred_element_type=jnp.float32)


def swap_groups(tiles):
    lane = lax.broadcasted_iota(jnp.int32, tiles[0].shape, 1)
    width = tiles[0].shape[1]
    half, quarter = width // 2, width // 4
    low, even = lane < half, lane // quarter % 2 == 0
    a = [
        jnp.where(low, tiles[0], pltpu.roll(tiles[2], half, 1)),
        jnp.where(low, tiles[1], pltpu.roll(tiles[3], half, 1)),
        jnp.where(low, pltpu.roll(tiles[0], half, 1), tiles[2]),
        jnp.where(low, pltpu.roll(tiles[1], half, 1), tiles[3]),
    ]
    return [
        jnp.where(even, a[0], pltpu.roll(a[1], quarter, 1)),
        jnp.where(even, pltpu.roll(a[0], width - quarter, 1), a[1]),
        jnp.where(even, a[2], pltpu.roll(a[3], quarter, 1)),
        jnp.where(even, pltpu.roll(a[2], width - quarter, 1), a[3]),
    ]


NEAR, FAR, WIDE = 9, 17, 137


def mix_kernel(places, back_places, mine, recv_ref, send_ref, got, partner, back):
    rows = len(places[0])
    depth = 4 * mine
    for col, column in enumerate(places):
        for row, place in enumerate(column):
            block = recv_ref[place].astype(jnp.float32)
            for high in range(2):
                for middle in range(2):
                    tile = block[8 * high : 8 * high + 8, 128 * middle : 128 * middle + 128]
                    got[col, 2 * high + middle, pl.ds(NEAR * row, 8, stride=FAR), :] = tile

    def side(which, channel):
        some = pl.ds(FAR * (which * mine + channel), rows, stride=NEAR)
        tiles = []
        for middle in range(2):
            some_of = [
                jnp.concatenate([got[col, middle, some, :], got[col, 2 + middle, some, :]], axis=0)
                for col in range(len(places))
            ]
            tiles += swap_groups([tile.astype(jnp.bfloat16) for tile in some_of])
        return tiles

    def spread_rows(target, first, step, tile):
        tile = tile.astype(jnp.float32)
        for high in range(2):
            some = pl.ds(NEAR * (first + high * step), rows, stride=WIDE)
            target[some, :] = tile[high * rows : (high + 1) * rows]

    channels = range(mine)
    for channel in channels:
        for n, tile in enumerate(side(1, channel)):
            spread_rows(partner.at[channel], n, 8, tile)
    lefts = [jnp.concatenate(side(0, channel), axis=0) for channel in channels]
    rights = [
        [
            partner[channel, pl.ds(WIDE * row + NEAR * n, 8, stride=NEAR), :]
            for row in range(rows)
            for n in (0, 8)
        ]
        for channel in channels
    ]
    rights = [jnp.concatenate(right, axis=0).astype(jnp.bfloat16) for right in rights]
    tris = [dot_t(left, right).astype(jnp.bfloat16) for left, right in zip(lefts, rights)]
    for channel, tri in enumerate(tris):
        for middle in range(2):
            firsts = [(4 * middle + n) * 2 * rows for n in range(4)]
            tiles = swap_groups([tri[first : first + 2 * rows] for first in firsts])
            for col, tile in enumerate(tiles):
                spread_rows(back.at[col], middle * mine + channel, 2 * mine, tile)
    for col, column in enumerate(back_places):
        for row, place in enumerate(column):
            tiles = [
                back[col, pl.ds(WIDE * row + NEAR * n, 8, stride=NEAR), :]
                for n in range(0, depth, 8)
            ]
            send_ref[place] = jnp.concatenate(tiles, axis=0).astype(jnp.bfloat16)


def finish_kernel(owners, recv_ref, normed_ref, gate_weight_ref, weight_ref, out_hbm, out_ref, done):
    devices, depth, width = recv_ref.shape
    values = jnp.stack([recv_ref[place] for place in owners]).astype(jnp.float32)
    values = values.reshape(devices // 2, 2, depth // 8, 8, width)
    top = lax.broadcasted_iota(jnp.int32, (devices // 2, 8, width), 1) < 4
    weight = weight_ref[...]
    gate = sigmoid(
        jnp.dot(normed_ref[...], gate_weight_ref[...], preferred_element_type=jnp.float32)
    )
    parts = []
    for n in range(depth // 8):
        one, two = values[:, 0, n], values[:, 1, n]
        parts.append(jnp.where(top, one, pltpu.roll(two, 4, 1)))
        parts.append(jnp.where(top, pltpu.roll(one, 4, 1), two))
    parts = [part.reshape(devices * 4, width) for part in parts]
    stats = []
    for part in parts:
        mean = jnp.mean(part, axis=0, keepdims=True)
        centred = part - mean
        var = jnp.mean(centred * centred, axis=0, keepdims=True)
        stats += [mean, jax.lax.rsqrt(var + 1e-05)]
    stats = jnp.concatenate(stats, axis=0).T
    total = jnp.sum(weight.astype(jnp.float32), axis=0, keepdims=True)
    copies = []
    for n, part in enumerate(parts):
        mean, scale = stats[:, 2 * n : 2 * n + 1], stats[:, 2 * n + 1 : 2 * n + 2]
        update = jnp.dot(part.T.astype(jnp.bfloat16), weight, preferred_element_type=jnp.float32)
        update = scale * (update - mean * total)
        spots = pl.ds(n * width, width)
        out_ref[spots, :] = (gate[n * width : (n + 1) * width] * update).astype(jnp.bfloat16)
        copies.append(pltpu.make_async_copy(out_ref.at[spots], out_hbm.at[spots], done.at[n]))
    for copy in copies:
        copy.start()
    for copy in copies:
        copy.wait()


def in_hbm(values):
    return pltpu.with_memory_space_constraint(values, pltpu.HBM)


def places_of(order):
    sizes = {name: lax.axis_size(name) for name in order}
    steps = {name: math.prod([sizes[n] for n in order[at + 1 :]]) for at, name in enumerate(order)}

    def offsets(slow, fast):
        pairs = [(m, n) for m in range(sizes[slow]) for n in range(sizes[fast])]
        return [m * steps[slow] + n * steps[fast] for m, n in pairs]

    return [[first + row for row in offsets("z", "core")] for first in offsets("y", "x")]


def split_channels(pair, pair_mask, in_weights, gate_weight, out_weight):
    rows_here, cols_here, width = pair.shape
    hidden = in_weights.shape[1] // 4
    places, back_places = places_of(THERE), places_of(BACK)
    rows, cols = len(places[0]), len(places)
    owners = sorted(zip(sum(places, []), sum(back_places, [])))
    devices = rows * cols
    mine = hidden // devices
    spots = rows_here * cols_here
    params = pltpu.CompilerParams(vmem_limit_bytes=32 * 2**20)
    both, normed = pl.pallas_call(
        functools.partial(project_kernel, devices, mine, cols_here),
        out_shape=(
            jax.ShapeDtypeStruct((devices, 4 * mine, spots // 2), jnp.bfloat16),
            jax.ShapeDtypeStruct((spots, width), jnp.bfloat16),
        ),
        in_specs=[pl.BlockSpec(memory_space=pltpu.HBM)] * 3,
        scratch_shapes=[
            pltpu.VMEM((spots, width), pair.dtype),
            pltpu.VMEM(pair_mask.shape, pair_mask.dtype),
            pltpu.VMEM(in_weights.shape, in_weights.dtype),
            pltpu.SemaphoreType.DMA((9,)),
        ],
        compiler_params=params,
        name="project",
    )(*(in_hbm(values) for values in (pair.reshape(spots, width), pair_mask, in_weights)))
    both = lax.all_to_all(both, THERE, 0, 0, tiled=True)
    tri = pl.pallas_call(
        functools.partial(mix_kernel, places, back_places, mine),
        out_shape=jax.ShapeDtypeStruct((devices, 4 * mine, spots // 4), jnp.bfloat16),
        scratch_shapes=[
            pltpu.VMEM((cols, 4, 184, 128), jnp.float32),
            pltpu.VMEM((mine, 1096, 128), jnp.float32),
            pltpu.VMEM((cols, 1096, 128), jnp.float32),
        ],
        compiler_params=params,
        name="mix",
    )(both)
    tri = lax.all_to_all(tri, BACK, 0, 0, tiled=True)
    update = pl.pallas_call(
        functools.partial(finish_kernel, [place for _, place in owners]),
        out_shape=jax.ShapeDtypeStruct((spots, width), jnp.bfloat16),
        out_specs=pl.BlockSpec(memory_space=pltpu.HBM),
        scratch_shapes=[pltpu.VMEM((spots, width), jnp.bfloat16), pltpu.SemaphoreType.DMA((4,))],
        compiler_params=params,
        name="finish",
    )(tri, normed, gate_weight, out_weight)
    return update.reshape(rows_here, cols_here, width)


def fits(rows, cols, pair, hidden):
    sizes = (rows, cols, pair.shape[0] // rows, pair.shape[1] // cols, pair.shape[2])
    return sizes == (8, 4, 16, 32, 128) and hidden == 4 * rows * cols


def solution(mesh):
    def update(pair, pair_mask, in_weights, gate_weight, out_weight):
        rows, cols = mesh.shape["row"], mesh.shape["col"]
        if fits(rows, cols, pair, in_weights.shape[1] // 4):
            plan, row, col = split_channels, ("z", "core"), ("y", "x")
            over = jax.sharding.Mesh(mesh.devices.reshape(rows // 2, 2, 2, cols // 2), row + col)
        else:
            plan, row, col, over = gather_rows, "row", "col", mesh
        in_specs = (P(row, col, None), P(row, col), P(), P(), P())
        out_specs = P(row, col, None)
        run = jax.shard_map(plan, mesh=over, in_specs=in_specs, out_specs=out_specs, check_vma=False)
        return run(pair, pair_mask, in_weights, gate_weight, out_weight)

    return update
```

```python
import functools
import math

import jax
import jax.numpy as jnp
from jax import lax
from jax.experimental import pallas as pl
from jax.experimental.pallas import tpu as pltpu
from jax.sharding import PartitionSpec as P

ORDER = ("core", "x", "y", "z")


def spread(value, axis, root):
    mine = lax.axis_index(axis) == root
    return lax.psum(jnp.where(mine, value, jnp.zeros_like(value)), axis)


def layer_norm(values, axis=-1):
    mean = jnp.mean(values, axis=axis, keepdims=True)
    centred = values - mean
    var = jnp.mean(centred * centred, axis=axis, keepdims=True)
    return centred * jax.lax.rsqrt(var + 1e-05)


def gather_rows(pair, pair_mask, in_weights, gate_weight, out_weight):
    rows_here = pair.shape[0]
    cols_here = pair.shape[1]
    width = pair.shape[2]
    hidden = in_weights.shape[1] // 4
    normed = layer_norm(pair.reshape(-1, width).astype(jnp.float32)).astype(jnp.bfloat16)
    proj = jnp.dot(normed, in_weights, preferred_element_type=jnp.float32)
    maskf = pair_mask.reshape(-1, 1).astype(jnp.float32)
    left = (maskf * jax.nn.sigmoid(proj[:, hidden : 2 * hidden]) * proj[:, :hidden]).astype(
        jnp.bfloat16
    )
    right = (
        maskf * jax.nn.sigmoid(proj[:, 3 * hidden :]) * proj[:, 2 * hidden : 3 * hidden]
    ).astype(jnp.bfloat16)
    left = left.reshape(rows_here, cols_here, hidden)
    right = right.reshape(rows_here, cols_here, hidden)
    gate = jax.nn.sigmoid(jnp.dot(normed, gate_weight, preferred_element_type=jnp.float32))
    ratio = lax.axis_size("row") // lax.axis_size("col")
    column = lax.axis_index("col")
    left_rows, right_rows = (
        lax.all_gather(left, "col", axis=1, tiled=True),
        lax.all_gather(right, "col", axis=1, tiled=True),
    )
    blocks = [spread(right_rows, "row", ratio * column + offset) for offset in range(ratio)]
    partner = jnp.concatenate(blocks, axis=0)
    tri = jnp.einsum("ikc,jkc->ijc", left_rows, partner, preferred_element_type=jnp.float32)
    tnorm = layer_norm(tri.reshape(-1, hidden)).astype(jnp.bfloat16)
    update = gate * jnp.dot(tnorm, out_weight, preferred_element_type=jnp.float32)
    return update.astype(jnp.bfloat16).reshape(rows_here, cols_here, width)


def sigmoid(values):
    return 0.5 * jnp.tanh(0.5 * values) + 0.5


def project_kernel(
    devices, mine, cols_here,
    pair_hbm, mask_hbm, weights_hbm, send_ref, normed_ref, pair_ref, mask_ref, weights_ref, done,
):
    spots, width = pair_ref.shape
    hidden = devices * mine
    copies = [(mask_hbm, mask_ref)]
    for source, target in ((weights_hbm, weights_ref), (pair_hbm, pair_ref)):
        part = source.shape[0] // 4
        parts = [pl.ds(n * part, part) for n in range(4)]
        copies += [(source.at[some], target.at[some]) for some in parts]
    copies = [pltpu.make_async_copy(*ends, done.at[n]) for n, ends in enumerate(copies)]
    for copy in copies:
        copy.start()
    shape = (2 * hidden, 2 * hidden)
    row, col = (lax.broadcasted_iota(jnp.int32, shape, n) for n in (0, 1))
    source = (row // mine) % 2 * hidden + row // (2 * mine) * mine + row % mine
    order = (col == source).astype(jnp.bfloat16)
    shape = (cols_here, spots)
    row, col = (lax.broadcasted_iota(jnp.int32, shape, n) for n in (0, 1))
    spread_cols = (col % cols_here == row).astype(jnp.bfloat16)
    shape = (spots // cols_here, spots)
    row, col = (lax.broadcasted_iota(jnp.int32, shape, n) for n in (0, 1))
    own = col // cols_here == row
    for copy in copies:
        copy.wait()
    weights = weights_ref[...]

    blocks = [weights[:, n * hidden : (n + 1) * hidden] for n in range(4)]
    pairs = [jnp.concatenate(blocks[n::2], axis=1) for n in range(2)]
    ordered = dot_t(order, jnp.concatenate(pairs, axis=0)).astype(jnp.bfloat16)
    ordered = jnp.concatenate([ordered[:, :width], ordered[:, width:]], axis=0)

    mask = mask_ref[...].astype(jnp.float32).astype(jnp.bfloat16)
    mask = jnp.dot(mask, spread_cols, preferred_element_type=jnp.float32)
    mask = jnp.sum(jnp.where(own, mask, 0.0), axis=0, keepdims=True)
    normed = layer_norm(pair_ref[...].astype(jnp.float32)).astype(jnp.bfloat16)
    normed_ref[...] = normed
    proj = dot_t(ordered, normed)
    both = mask * sigmoid(proj[2 * hidden :]) * proj[: 2 * hidden]
    both = both.reshape(devices, 2 * mine, spots)
    half = spots // 2
    both = jnp.concatenate([both[:, :, :half], both[:, :, half:]], axis=1)
    send_ref[...] = both.astype(jnp.bfloat16)


def dot_t(a, b):
    return lax.dot_general(a, b, (((1,), (1,)), ((), ())), preferred_element_type=jnp.float32)


def swap_groups(tiles):
    lane = lax.broadcasted_iota(jnp.int32, tiles[0].shape, 1)
    width = tiles[0].shape[1]
    half, quarter = width // 2, width // 4
    low, even = lane < half, lane // quarter % 2 == 0
    a = [
        jnp.where(low, tiles[0], pltpu.roll(tiles[2], half, 1)),
        jnp.where(low, tiles[1], pltpu.roll(tiles[3], half, 1)),
        jnp.where(low, pltpu.roll(tiles[0], half, 1), tiles[2]),
        jnp.where(low, pltpu.roll(tiles[1], half, 1), tiles[3]),
    ]
    return [
        jnp.where(even, a[0], pltpu.roll(a[1], quarter, 1)),
        jnp.where(even, pltpu.roll(a[0], width - quarter, 1), a[1]),
        jnp.where(even, a[2], pltpu.roll(a[3], quarter, 1)),
        jnp.where(even, pltpu.roll(a[2], width - quarter, 1), a[3]),
    ]


NEAR, FAR, WIDE = 9, 17, 137


def mix_kernel(places, mine, recv_ref, send_ref, got, partner, back):
    rows = len(places[0])
    depth = 4 * mine
    for col, column in enumerate(places):
        for row, place in enumerate(column):
            block = recv_ref[place].astype(jnp.float32)
            for high in range(2):
                for middle in range(2):
                    tile = block[8 * high : 8 * high + 8, 128 * middle : 128 * middle + 128]
                    got[col, 2 * high + middle, pl.ds(NEAR * row, 8, stride=FAR), :] = tile

    def side(which, channel):
        some = pl.ds(FAR * (which * mine + channel), rows, stride=NEAR)
        tiles = []
        for middle in range(2):
            some_of = [
                jnp.concatenate([got[col, middle, some, :], got[col, 2 + middle, some, :]], axis=0)
                for col in range(len(places))
            ]
            tiles += swap_groups([tile.astype(jnp.bfloat16) for tile in some_of])
        return tiles

    def spread_rows(target, first, step, tile):
        tile = tile.astype(jnp.float32)
        for high in range(2):
            some = pl.ds(NEAR * (first + high * step), rows, stride=WIDE)
            target[some, :] = tile[high * rows : (high + 1) * rows]

    channels = range(mine)
    for channel in channels:
        for n, tile in enumerate(side(1, channel)):
            spread_rows(partner.at[channel], n, 8, tile)
    lefts = [jnp.concatenate(side(0, channel), axis=0) for channel in channels]
    rights = [
        [
            partner[channel, pl.ds(WIDE * row + NEAR * n, 8, stride=NEAR), :]
            for row in range(rows)
            for n in (0, 8)
        ]
        for channel in channels
    ]
    rights = [jnp.concatenate(right, axis=0).astype(jnp.bfloat16) for right in rights]
    tris = [dot_t(left, right).astype(jnp.bfloat16) for left, right in zip(lefts, rights)]
    for channel, tri in enumerate(tris):
        for middle in range(2):
            firsts = [(4 * middle + n) * 2 * rows for n in range(4)]
            tiles = swap_groups([tri[first : first + 2 * rows] for first in firsts])
            for col, tile in enumerate(tiles):
                spread_rows(back.at[col], middle * mine + channel, 2 * mine, tile)
    for col, column in enumerate(places):
        for row, place in enumerate(column):
            tiles = [
                back[col, pl.ds(WIDE * row + NEAR * n, 8, stride=NEAR), :]
                for n in range(0, depth, 8)
            ]
            send_ref[place] = jnp.concatenate(tiles, axis=0).astype(jnp.bfloat16)


def finish_kernel(recv_ref, normed_ref, gate_weight_ref, weight_ref, out_hbm, out_ref, done):
    devices, depth, width = recv_ref.shape
    values = recv_ref[...].astype(jnp.float32).reshape(devices // 2, 2, depth // 8, 8, width)
    top = lax.broadcasted_iota(jnp.int32, (devices // 2, 8, width), 1) < 4
    weight = weight_ref[...]
    gate = sigmoid(
        jnp.dot(normed_ref[...], gate_weight_ref[...], preferred_element_type=jnp.float32)
    )
    parts = []
    for n in range(depth // 8):
        one, two = values[:, 0, n], values[:, 1, n]
        parts.append(jnp.where(top, one, pltpu.roll(two, 4, 1)))
        parts.append(jnp.where(top, pltpu.roll(one, 4, 1), two))
    parts = [layer_norm(part.reshape(devices * 4, width), axis=0).T for part in parts]
    tnorm = jnp.concatenate(parts, axis=0).astype(jnp.bfloat16)
    update = jnp.dot(tnorm, weight, preferred_element_type=jnp.float32)
    out_ref[...] = (gate * update).astype(jnp.bfloat16)
    copies = []
    for n in range(len(parts)):
        spots = pl.ds(n * width, width)
        copies.append(pltpu.make_async_copy(out_ref.at[spots], out_hbm.at[spots], done.at[n]))
    for copy in copies:
        copy.start()
    for copy in copies:
        copy.wait()


def in_hbm(values):
    return pltpu.with_memory_space_constraint(values, pltpu.HBM)


def split_channels(pair, pair_mask, in_weights, gate_weight, out_weight):
    rows_here, cols_here, width = pair.shape
    hidden = in_weights.shape[1] // 4
    sizes = {name: lax.axis_size(name) for name in ORDER}
    steps = {name: math.prod([sizes[n] for n in ORDER[at + 1 :]]) for at, name in enumerate(ORDER)}

    def offsets(slow, fast):
        pairs = [(m, n) for m in range(sizes[slow]) for n in range(sizes[fast])]
        return [m * steps[slow] + n * steps[fast] for m, n in pairs]

    in_rows, in_cols = offsets("z", "core"), offsets("y", "x")
    places = [[first + row for row in in_rows] for first in in_cols]
    rows, cols = len(in_rows), len(in_cols)
    devices = rows * cols
    mine = hidden // devices
    spots = rows_here * cols_here
    params = pltpu.CompilerParams(vmem_limit_bytes=32 * 2**20)
    both, normed = pl.pallas_call(
        functools.partial(project_kernel, devices, mine, cols_here),
        out_shape=(
            jax.ShapeDtypeStruct((devices, 4 * mine, spots // 2), jnp.bfloat16),
            jax.ShapeDtypeStruct((spots, width), jnp.bfloat16),
        ),
        in_specs=[pl.BlockSpec(memory_space=pltpu.HBM)] * 3,
        scratch_shapes=[
            pltpu.VMEM((spots, width), pair.dtype),
            pltpu.VMEM(pair_mask.shape, pair_mask.dtype),
            pltpu.VMEM(in_weights.shape, in_weights.dtype),
            pltpu.SemaphoreType.DMA((9,)),
        ],
        compiler_params=params,
        name="project",
    )(*(in_hbm(values) for values in (pair.reshape(spots, width), pair_mask, in_weights)))
    both = lax.all_to_all(both, ORDER, 0, 0, tiled=True)
    tri = pl.pallas_call(
        functools.partial(mix_kernel, places, mine),
        out_shape=jax.ShapeDtypeStruct((devices, 4 * mine, spots // 4), jnp.bfloat16),
        scratch_shapes=[
            pltpu.VMEM((cols, 4, 184, 128), jnp.float32),
            pltpu.VMEM((mine, 1096, 128), jnp.float32),
            pltpu.VMEM((cols, 1096, 128), jnp.float32),
        ],
        compiler_params=params,
        name="mix",
    )(both)
    tri = lax.all_to_all(tri, ORDER, 0, 0, tiled=True)
    update = pl.pallas_call(
        finish_kernel,
        out_shape=jax.ShapeDtypeStruct((spots, width), jnp.bfloat16),
        out_specs=pl.BlockSpec(memory_space=pltpu.HBM),
        scratch_shapes=[pltpu.VMEM((spots, width), jnp.bfloat16), pltpu.SemaphoreType.DMA((4,))],
        compiler_params=params,
        name="finish",
    )(tri, normed, gate_weight, out_weight)
    return update.reshape(rows_here, cols_here, width)


def fits(rows, cols, pair, hidden):
    sizes = (rows, cols, pair.shape[0] // rows, pair.shape[1] // cols, pair.shape[2])
    return sizes == (8, 4, 16, 32, 128) and hidden == 4 * rows * cols


def solution(mesh):
    def update(pair, pair_mask, in_weights, gate_weight, out_weight):
        rows, cols = mesh.shape["row"], mesh.shape["col"]
        if fits(rows, cols, pair, in_weights.shape[1] // 4):
            plan, row, col = split_channels, ("z", "core"), ("y", "x")
            over = jax.sharding.Mesh(mesh.devices.reshape(rows // 2, 2, 2, cols // 2), row + col)
        else:
            plan, row, col, over = gather_rows, "row", "col", mesh
        in_specs = (P(row, col, None), P(row, col), P(), P(), P())
        out_specs = P(row, col, None)
        run = jax.shard_map(plan, mesh=over, in_specs=in_specs, out_specs=out_specs, check_vma=False)
        return run(pair, pair_mask, in_weights, gate_weight, out_weight)

    return update
```

```python
import functools
import math

import jax
import jax.numpy as jnp
from jax import lax
from jax.experimental import pallas as pl
from jax.experimental.pallas import tpu as pltpu
from jax.sharding import PartitionSpec as P

ORDER = ("core", "x", "y", "z")


def spread(value, axis, root):
    mine = lax.axis_index(axis) == root
    return lax.psum(jnp.where(mine, value, jnp.zeros_like(value)), axis)


def layer_norm(values, axis=-1):
    mean = jnp.mean(values, axis=axis, keepdims=True)
    centred = values - mean
    var = jnp.mean(centred * centred, axis=axis, keepdims=True)
    return centred * jax.lax.rsqrt(var + 1e-05)


def gather_rows(pair, pair_mask, in_weights, gate_weight, out_weight):
    rows_here = pair.shape[0]
    cols_here = pair.shape[1]
    width = pair.shape[2]
    hidden = in_weights.shape[1] // 4
    normed = layer_norm(pair.reshape(-1, width).astype(jnp.float32)).astype(jnp.bfloat16)
    proj = jnp.dot(normed, in_weights, preferred_element_type=jnp.float32)
    maskf = pair_mask.reshape(-1, 1).astype(jnp.float32)
    left = (maskf * jax.nn.sigmoid(proj[:, hidden : 2 * hidden]) * proj[:, :hidden]).astype(
        jnp.bfloat16
    )
    right = (
        maskf * jax.nn.sigmoid(proj[:, 3 * hidden :]) * proj[:, 2 * hidden : 3 * hidden]
    ).astype(jnp.bfloat16)
    left = left.reshape(rows_here, cols_here, hidden)
    right = right.reshape(rows_here, cols_here, hidden)
    gate = jax.nn.sigmoid(jnp.dot(normed, gate_weight, preferred_element_type=jnp.float32))
    ratio = lax.axis_size("row") // lax.axis_size("col")
    column = lax.axis_index("col")
    left_rows, right_rows = (
        lax.all_gather(left, "col", axis=1, tiled=True),
        lax.all_gather(right, "col", axis=1, tiled=True),
    )
    blocks = [spread(right_rows, "row", ratio * column + offset) for offset in range(ratio)]
    partner = jnp.concatenate(blocks, axis=0)
    tri = jnp.einsum("ikc,jkc->ijc", left_rows, partner, preferred_element_type=jnp.float32)
    tnorm = layer_norm(tri.reshape(-1, hidden)).astype(jnp.bfloat16)
    update = gate * jnp.dot(tnorm, out_weight, preferred_element_type=jnp.float32)
    return update.astype(jnp.bfloat16).reshape(rows_here, cols_here, width)


def sigmoid(values):
    return 0.5 * jnp.tanh(0.5 * values) + 0.5


def project_kernel(
    devices, mine, cols_here,
    pair_hbm, mask_hbm, weights_hbm, send_ref, normed_ref, pair_ref, mask_ref, weights_ref, done,
):
    spots, width = pair_ref.shape
    hidden = devices * mine
    copies = [(mask_hbm, mask_ref)]
    for source, target in ((weights_hbm, weights_ref), (pair_hbm, pair_ref)):
        part = source.shape[0] // 4
        parts = [pl.ds(n * part, part) for n in range(4)]
        copies += [(source.at[some], target.at[some]) for some in parts]
    copies = [pltpu.make_async_copy(*ends, done.at[n]) for n, ends in enumerate(copies)]
    for n, copy in enumerate(copies):
        copy.start(priority=n % 2)
    shape = (2 * hidden, 2 * hidden)
    row, col = (lax.broadcasted_iota(jnp.int32, shape, n) for n in (0, 1))
    source = (row // mine) % 2 * hidden + row // (2 * mine) * mine + row % mine
    order = (col == source).astype(jnp.bfloat16)
    shape = (cols_here, spots)
    row, col = (lax.broadcasted_iota(jnp.int32, shape, n) for n in (0, 1))
    spread_cols = (col % cols_here == row).astype(jnp.bfloat16)
    shape = (spots // cols_here, spots)
    row, col = (lax.broadcasted_iota(jnp.int32, shape, n) for n in (0, 1))
    own = col // cols_here == row
    for copy in copies:
        copy.wait()
    weights = weights_ref[...]

    blocks = [weights[:, n * hidden : (n + 1) * hidden] for n in range(4)]
    pairs = [jnp.concatenate(blocks[n::2], axis=1) for n in range(2)]
    ordered = dot_t(order, jnp.concatenate(pairs, axis=0)).astype(jnp.bfloat16)
    ordered = jnp.concatenate([ordered[:, :width], ordered[:, width:]], axis=0)

    mask = mask_ref[...].astype(jnp.float32).astype(jnp.bfloat16)
    mask = jnp.dot(mask, spread_cols, preferred_element_type=jnp.float32)
    mask = jnp.sum(jnp.where(own, mask, 0.0), axis=0, keepdims=True)
    normed = layer_norm(pair_ref[...].astype(jnp.float32)).astype(jnp.bfloat16)
    normed_ref[...] = normed
    proj = dot_t(ordered, normed)
    both = mask * sigmoid(proj[2 * hidden :]) * proj[: 2 * hidden]
    both = both.reshape(devices, 2 * mine, spots)
    half = spots // 2
    both = jnp.concatenate([both[:, :, :half], both[:, :, half:]], axis=1)
    send_ref[...] = both.astype(jnp.bfloat16)


def dot_t(a, b):
    return lax.dot_general(a, b, (((1,), (1,)), ((), ())), preferred_element_type=jnp.float32)


def swap_groups(tiles):
    lane = lax.broadcasted_iota(jnp.int32, tiles[0].shape, 1)
    width = tiles[0].shape[1]
    half, quarter = width // 2, width // 4
    low, even = lane < half, lane // quarter % 2 == 0
    a = [
        jnp.where(low, tiles[0], pltpu.roll(tiles[2], half, 1)),
        jnp.where(low, tiles[1], pltpu.roll(tiles[3], half, 1)),
        jnp.where(low, pltpu.roll(tiles[0], half, 1), tiles[2]),
        jnp.where(low, pltpu.roll(tiles[1], half, 1), tiles[3]),
    ]
    return [
        jnp.where(even, a[0], pltpu.roll(a[1], quarter, 1)),
        jnp.where(even, pltpu.roll(a[0], width - quarter, 1), a[1]),
        jnp.where(even, a[2], pltpu.roll(a[3], quarter, 1)),
        jnp.where(even, pltpu.roll(a[2], width - quarter, 1), a[3]),
    ]


NEAR, FAR, WIDE = 9, 17, 137


def mix_kernel(places, mine, recv_ref, send_ref, got, partner, back):
    rows = len(places[0])
    depth = 4 * mine
    for col, column in enumerate(places):
        for row, place in enumerate(column):
            block = recv_ref[place].astype(jnp.float32)
            for high in range(2):
                for middle in range(2):
                    tile = block[8 * high : 8 * high + 8, 128 * middle : 128 * middle + 128]
                    got[col, 2 * high + middle, pl.ds(NEAR * row, 8, stride=FAR), :] = tile

    def side(which, channel):
        some = pl.ds(FAR * (which * mine + channel), rows, stride=NEAR)
        tiles = []
        for middle in range(2):
            some_of = [
                jnp.concatenate([got[col, middle, some, :], got[col, 2 + middle, some, :]], axis=0)
                for col in range(len(places))
            ]
            tiles += swap_groups([tile.astype(jnp.bfloat16) for tile in some_of])
        return tiles

    def spread_rows(target, first, step, tile):
        tile = tile.astype(jnp.float32)
        for high in range(2):
            some = pl.ds(NEAR * (first + high * step), rows, stride=WIDE)
            target[some, :] = tile[high * rows : (high + 1) * rows]

    channels = range(mine)
    for channel in channels:
        for n, tile in enumerate(side(1, channel)):
            spread_rows(partner.at[channel], n, 8, tile)
    lefts = [jnp.concatenate(side(0, channel), axis=0) for channel in channels]
    rights = [
        [
            partner[channel, pl.ds(WIDE * row + NEAR * n, 8, stride=NEAR), :]
            for row in range(rows)
            for n in (0, 8)
        ]
        for channel in channels
    ]
    rights = [jnp.concatenate(right, axis=0).astype(jnp.bfloat16) for right in rights]
    tris = [dot_t(left, right).astype(jnp.bfloat16) for left, right in zip(lefts, rights)]
    for channel, tri in enumerate(tris):
        for middle in range(2):
            firsts = [(4 * middle + n) * 2 * rows for n in range(4)]
            tiles = swap_groups([tri[first : first + 2 * rows] for first in firsts])
            for col, tile in enumerate(tiles):
                spread_rows(back.at[col], middle * mine + channel, 2 * mine, tile)
    for col, column in enumerate(places):
        for row, place in enumerate(column):
            tiles = [
                back[col, pl.ds(WIDE * row + NEAR * n, 8, stride=NEAR), :]
                for n in range(0, depth, 8)
            ]
            send_ref[place] = jnp.concatenate(tiles, axis=0).astype(jnp.bfloat16)


def finish_kernel(recv_ref, normed_ref, gate_weight_ref, weight_ref, out_hbm, out_ref, done):
    devices, depth, width = recv_ref.shape
    values = recv_ref[...].astype(jnp.float32).reshape(devices // 2, 2, depth // 8, 8, width)
    top = lax.broadcasted_iota(jnp.int32, (devices // 2, 8, width), 1) < 4
    weight = weight_ref[...]
    gate = sigmoid(
        jnp.dot(normed_ref[...], gate_weight_ref[...], preferred_element_type=jnp.float32)
    )
    parts = []
    for n in range(depth // 8):
        one, two = values[:, 0, n], values[:, 1, n]
        parts.append(jnp.where(top, one, pltpu.roll(two, 4, 1)))
        parts.append(jnp.where(top, pltpu.roll(one, 4, 1), two))
    parts = [layer_norm(part.reshape(devices * 4, width), axis=0).T for part in parts]
    tnorm = jnp.concatenate(parts, axis=0).astype(jnp.bfloat16)
    update = jnp.dot(tnorm, weight, preferred_element_type=jnp.float32)
    out_ref[...] = (gate * update).astype(jnp.bfloat16)
    copies = []
    for n in range(len(parts)):
        spots = pl.ds(n * width, width)
        copies.append(pltpu.make_async_copy(out_ref.at[spots], out_hbm.at[spots], done.at[n]))
    for n, copy in enumerate(copies):
        copy.start(priority=n % 2)
    for copy in copies:
        copy.wait()


def in_hbm(values):
    return pltpu.with_memory_space_constraint(values, pltpu.HBM)


def split_channels(pair, pair_mask, in_weights, gate_weight, out_weight):
    rows_here, cols_here, width = pair.shape
    hidden = in_weights.shape[1] // 4
    sizes = {name: lax.axis_size(name) for name in ORDER}
    steps = {name: math.prod([sizes[n] for n in ORDER[at + 1 :]]) for at, name in enumerate(ORDER)}

    def offsets(slow, fast):
        pairs = [(m, n) for m in range(sizes[slow]) for n in range(sizes[fast])]
        return [m * steps[slow] + n * steps[fast] for m, n in pairs]

    in_rows, in_cols = offsets("z", "core"), offsets("y", "x")
    places = [[first + row for row in in_rows] for first in in_cols]
    rows, cols = len(in_rows), len(in_cols)
    devices = rows * cols
    mine = hidden // devices
    spots = rows_here * cols_here
    params = pltpu.CompilerParams(vmem_limit_bytes=32 * 2**20)
    both, normed = pl.pallas_call(
        functools.partial(project_kernel, devices, mine, cols_here),
        out_shape=(
            jax.ShapeDtypeStruct((devices, 4 * mine, spots // 2), jnp.bfloat16),
            jax.ShapeDtypeStruct((spots, width), jnp.bfloat16),
        ),
        in_specs=[pl.BlockSpec(memory_space=pltpu.HBM)] * 3,
        scratch_shapes=[
            pltpu.VMEM((spots, width), pair.dtype),
            pltpu.VMEM(pair_mask.shape, pair_mask.dtype),
            pltpu.VMEM(in_weights.shape, in_weights.dtype),
            pltpu.SemaphoreType.DMA((9,)),
        ],
        compiler_params=params,
        name="project",
    )(*(in_hbm(values) for values in (pair.reshape(spots, width), pair_mask, in_weights)))
    both = lax.all_to_all(both, ORDER, 0, 0, tiled=True)
    tri = pl.pallas_call(
        functools.partial(mix_kernel, places, mine),
        out_shape=jax.ShapeDtypeStruct((devices, 4 * mine, spots // 4), jnp.bfloat16),
        scratch_shapes=[
            pltpu.VMEM((cols, 4, 184, 128), jnp.float32),
            pltpu.VMEM((mine, 1096, 128), jnp.float32),
            pltpu.VMEM((cols, 1096, 128), jnp.float32),
        ],
        compiler_params=params,
        name="mix",
    )(both)
    tri = lax.all_to_all(tri, ORDER, 0, 0, tiled=True)
    update = pl.pallas_call(
        finish_kernel,
        out_shape=jax.ShapeDtypeStruct((spots, width), jnp.bfloat16),
        out_specs=pl.BlockSpec(memory_space=pltpu.HBM),
        scratch_shapes=[pltpu.VMEM((spots, width), jnp.bfloat16), pltpu.SemaphoreType.DMA((4,))],
        compiler_params=params,
        name="finish",
    )(tri, normed, gate_weight, out_weight)
    return update.reshape(rows_here, cols_here, width)


def fits(rows, cols, pair, hidden):
    sizes = (rows, cols, pair.shape[0] // rows, pair.shape[1] // cols, pair.shape[2])
    return sizes == (8, 4, 16, 32, 128) and hidden == 4 * rows * cols


def solution(mesh):
    def update(pair, pair_mask, in_weights, gate_weight, out_weight):
        rows, cols = mesh.shape["row"], mesh.shape["col"]
        if fits(rows, cols, pair, in_weights.shape[1] // 4):
            plan, row, col = split_channels, ("z", "core"), ("y", "x")
            over = jax.sharding.Mesh(mesh.devices.reshape(rows // 2, 2, 2, cols // 2), row + col)
        else:
            plan, row, col, over = gather_rows, "row", "col", mesh
        in_specs = (P(row, col, None), P(row, col), P(), P(), P())
        out_specs = P(row, col, None)
        run = jax.shard_map(plan, mesh=over, in_specs=in_specs, out_specs=out_specs, check_vma=False)
        return run(pair, pair_mask, in_weights, gate_weight, out_weight)

    return update
```
